256 devices in a mesh: gx: 16 (over z, x_lo), gy: 8 (over y, x_hi), col: 2 (over core).
Axes of the slice: x: 4 (x_hi: 2, x_lo: 2; x = x_hi * 2 + x_lo), y: 4, z: 8, core: 2. Of those that a mesh axis runs over, the one named last changes fastest.
Arguments:
- source: float32 [256, 128, 512], P('gx', 'gy', 'col'), may hold values from -6 to 6
- conductance: float32 [256, 128, 512], P('gx', 'gy', 'col'), may hold values from 0.5 to 2
Outputs:
- solution: float32 [256, 128, 512], P('gx', 'gy', 'col')
- residual: float32 [256, 128, 512], P('gx', 'gy', 'col')
The draws below stay inside these ranges and needn't reach their ends.
All inputs are finite; a program needn't handle non-finite values.
Results may differ from the reference program's by a relative error of at most 0.0003.
Values sent between devices are 32-bit elements; how exact they have to be, the bound alone decides.
A program may use at most 64 MiB of HBM per device.

```python
import math
import jax
import jax.numpy as jnp

AGG = 16
DEGREE = 3
VISITS = 3
CCYC = 4
NX = 256
NY = 128
NZ = 512


def level_of(stream_key, extent, split, low, high):
    level, own = 1.0, jax.random.fold_in(stream_key, 6)
    for dim, shards_of in split:
        heights = jnp.exp(jax.random.uniform(jax.random.fold_in(own, dim), (shards_of,), jnp.float32, low / len(split), high / len(split)))
        level = level * jnp.repeat(heights, extent[dim] // shards_of).reshape([-1 if axis == dim else 1 for axis in range(len(extent))])
    return level


def bell_draw(stream_key, shape, scale, bound, split=(), kind=jnp.bfloat16):
    gain = level_of(stream_key, shape, split, -0.22, 0.18) if split else 1.0
    array = jax.random.normal(stream_key, shape, jnp.float32) * scale * gain
    return jnp.minimum(jnp.maximum(array, -bound), bound).astype(kind)


def setup_inputs(seed: int = 0) -> dict:
    splits = jax.random.split(jax.random.key(seed), 3)
    return {
        "source": bell_draw(splits[0], (NX, NY, NZ), 1.0, 6.0, ((0, 16), (1, 8), (2, 2)), jnp.float32),
        "conductance": jnp.clip(jnp.exp(math.log(2.0) - 1.3862944 * jax.random.uniform(splits[1], (NX, NY, NZ), jnp.float32) ** level_of(splits[1], (NX, NY, NZ), ((0, 16), (1, 8), (2, 2)), -0.2, 0.2)), 0.5, 2.0),
    }


shift_term = 0.05
center_weight = 7.0 + shift_term
upper_bound = (8.0 + shift_term) / center_weight
fine_lower = upper_bound / 4.0
coarse_lower = shift_term / center_weight
prolong_weight = 0.5


def smooth_sum(padded):
    padded = 0.5 * padded[:-2] + padded[1:-1] + 0.5 * padded[2:]
    padded = 0.5 * padded[:, :-2] + padded[:, 1:-1] + 0.5 * padded[:, 2:]
    padded = 0.5 * padded[:, :, :-2] + padded[:, :, 1:-1] + 0.5 * padded[:, :, 2:]
    return padded


def apply_operator(field, coefficient):
    weighted = coefficient * field
    padded = jnp.pad(weighted, 1)
    return coefficient * ((8.0 + shift_term) * weighted - smooth_sum(padded))


def chebyshev(remainder, coefficient, lower, upper):
    theta_mid = (upper + lower) / 2.0
    half_width = (upper - lower) / 2.0
    sigma_ratio = theta_mid / half_width
    ratio_old = 1.0 / sigma_ratio
    inverse_diag = 1.0 / (center_weight * coefficient * coefficient)
    direction = inverse_diag * remainder / theta_mid
    correction = direction
    for step in range(DEGREE - 1):
        remainder = remainder - apply_operator(direction, coefficient)
        ratio_new = 1.0 / (2.0 * sigma_ratio - ratio_old)
        direction = ratio_new * ratio_old * direction + (2.0 * ratio_new / half_width) * inverse_diag * remainder
        correction = correction + direction
        ratio_old = ratio_new
    return correction


def block_sum(field):
    first, second, third = field.shape
    return field.reshape(first // AGG, AGG, second // AGG, AGG, third // AGG, AGG).sum(axis=(1, 3, 5))


def block_mean(field):
    first, second, third = field.shape
    return field.reshape(first // AGG, AGG, second // AGG, AGG, third // AGG, AGG).mean(axis=(1, 3, 5))


def prolong(coarse):
    first, second, third = coarse.shape
    spread = jnp.broadcast_to(coarse[:, None, :, None, :, None], (first, AGG, second, AGG, third, AGG))
    return spread.reshape(first * AGG, second * AGG, third * AGG)


def reference(source, conductance):
    coarse_cond = block_mean(conductance)
    solution = jnp.zeros_like(source)
    for visit in range(VISITS):
        if visit == 0:
            remainder = source
        else:
            remainder = source - apply_operator(solution, conductance)
        fine_part = chebyshev(remainder, conductance, fine_lower, upper_bound)
        coarse_rhs = block_sum(remainder) * (AGG ** -1.5)
        coarse_error = jnp.zeros_like(coarse_rhs)
        for cycle in range(CCYC):
            if cycle == 0:
                coarse_rem = coarse_rhs
            else:
                coarse_rem = coarse_rhs - apply_operator(coarse_error, coarse_cond)
            coarse_error = coarse_error + chebyshev(coarse_rem, coarse_cond, coarse_lower, upper_bound)
        solution = solution + fine_part + prolong_weight * prolong(coarse_error)
    residual = source - apply_operator(solution, conductance)
    return solution, residual
```

```python
import functools
import math

import jax
import jax.numpy as jnp
import numpy as np
from jax import lax
from jax.experimental import pallas as pl
from jax.experimental.pallas import tpu as pltpu
from jax.sharding import PartitionSpec as P

AGG = 16
DEGREE = 3
VISITS = 3
CCYC = 4

SHIFT = 0.05
CENTER = 7.0 + SHIFT
UPPER = (8.0 + SHIFT) / CENTER
FINE_LOWER = UPPER / 4.0
COARSE_LOWER = SHIFT / CENTER
PROLONG = 0.5

NB = 16
NL = 256
W = 3
NS = NB + 2 * W
NR = 24
NW = 384
MESH = pl.DeviceIdType.MESH
HIGH = lax.Precision.HIGHEST


def cheb_poly(lower, upper):
    theta, delta = (upper + lower) / 2.0, (upper - lower) / 2.0
    sigma = theta / delta
    rho = 1.0 / sigma
    op = np.poly1d([-1.0, 8.0 + SHIFT])
    rem = np.poly1d([1.0])
    direction = rem * (1.0 / (CENTER * theta))
    total = direction
    for _ in range(DEGREE - 1):
        rem = rem - op * direction
        rho_new = 1.0 / (2.0 * sigma - rho)
        direction = (rho_new * rho) * direction + (2.0 * rho_new / delta / CENTER) * rem
        total = total + direction
        rho = rho_new
    return total


def coarse_gain(lam):
    c = cheb_poly(COARSE_LOWER, UPPER)(lam)
    err = np.zeros_like(lam)
    for _ in range(CCYC):
        err = err + c * (1.0 - (8.0 + SHIFT - lam) * err)
    return err


def sine(n):
    k = np.arange(1, n + 1)
    v = math.sqrt(2.0 / (n + 1)) * np.sin(np.pi * np.outer(k, k) / (n + 1))
    return v, 1.0 + np.cos(np.pi * k / (n + 1))


def coarse_constants(gx, gy, cz):
    vx, lx = sine(gx)
    vy, ly = sine(gy)
    vz, lz = sine(cz)
    nxh = gx // 8
    order = [(xh * 8 + xl, y) for xl in range(8) for y in range(gy) for xh in range(nxh)]
    xs = np.array([o[0] for o in order])
    ys = np.array([o[1] for o in order])
    n = len(order)
    vyx = vx[np.ix_(xs, xs)] * vy[np.ix_(ys, ys)]
    lam = (lx[xs] * ly[ys])[:, None] * lz[None, :]
    gain = np.zeros((n, 128))
    gain[:, :cz] = PROLONG * AGG ** (-1.5) * coarse_gain(lam)
    vzp = np.zeros((128, 128))
    vzp[:cz, :cz] = vz
    where = {o: i for i, o in enumerate(order)}
    table = np.zeros((gx, gy, 32, n))
    for x in range(gx):
        for y in range(gy):
            for dx in range(3):
                for dy in range(3):
                    at = where.get((x + dx - 1, y + dy - 1))
                    if at is not None:
                        table[x, y, dx * 3 + dy] = vyx[at]
                        table[x, y, 16 + dx * 3 + dy, at] = 1.0
    f32 = np.float32
    return vyx.astype(f32), vzp.astype(f32), gain.astype(f32), table.reshape(gx * gy, 32, n).astype(f32)


def dot(a, b):
    return jnp.dot(a, b, precision=HIGH, preferred_element_type=jnp.float32)


def yz_sum(v):
    v = v + pltpu.roll(v, v.shape[0] - 1, 0)
    v = v + pltpu.roll(v, 1, 0)
    v = v + pltpu.roll(v, v.shape[1] - 1, 1)
    return v + pltpu.roll(v, 1, 1)


def stencil(load, emit, first, count, group):
    before = yz_sum(load(first - 1))
    here = yz_sum(load(first))

    def body(i, carry):
        pair, here = carry
        for k in range(group):
            s = first + i * group + k
            after = yz_sum(load(s + 1))
            pair_after = here + after
            emit(s, pair + pair_after)
            pair, here = pair_after, after
        return pair, here

    lax.fori_loop(0, count // group, body, (before + here, here))


def kernel(
    size,
    src_hbm, q_hbm, vyx_hbm, vz_hbm, gain_hbm, tab_hbm,
    sol_ref, res_ref,
    src, q, vyx, vz, gain, tab,
    field, qf, one, two, total, expanded, part, sums,
    ysend, yrecv, csend, crecv, zsend, zrecv,
    g1, g2, rv, qcinv, qcsel,
    lsem, hsend, hrecv, gsend, grecv,
):
    gxn, gyn, coln = size
    nxh = gxn // 8
    gx, gy, col = lax.axis_index("gx"), lax.axis_index("gy"), lax.axis_index("col")
    other = 1 - col
    poly = cheb_poly(FINE_LOWER, UPPER).coeffs
    c2, c1, c0 = (float(c) * 8.0**-k for c, k in zip(poly, (2, 1, 0)))

    locals_ = [
        pltpu.make_async_copy(src_hbm, src, lsem.at[0]),
        pltpu.make_async_copy(q_hbm, q, lsem.at[1]),
        pltpu.make_async_copy(tab_hbm.at[gx * gyn + gy], tab, lsem.at[2]),
        pltpu.make_async_copy(vyx_hbm, vyx, lsem.at[3]),
        pltpu.make_async_copy(vz_hbm, vz, lsem.at[4]),
        pltpu.make_async_copy(gain_hbm, gain, lsem.at[5]),
    ]
    for c in locals_:
        c.start()

    row_peers = [(lax.rem(gx + d, gxn), gy, col) for d in range(1, gxn)]
    plane_peers = [
        (gx, lax.rem(gy + dy, gyn), lax.rem(col + dc, coln))
        for dy in range(gyn) for dc in range(coln) if dy or dc
    ]
    xs = (lax.rem(gx + gxn - 1, gxn), lax.rem(gx + 1, gxn))
    ys = (lax.rem(gy + gyn - 1, gyn), lax.rem(gy + 1, gyn))
    corners = [(xs[a], ys[b], col) for a in range(2) for b in range(2)]
    barrier = pltpu.get_barrier_semaphore()
    peers = row_peers + plane_peers + corners
    for p in peers:
        pl.semaphore_signal(barrier, inc=1, device_id=p, device_id_type=MESH)

    one_f = jnp.float32(1.0)
    zero_f = jnp.float32(0.0)
    x_in = (jnp.where(gx > 0, one_f, zero_f), jnp.where(gx < gxn - 1, one_f, zero_f))
    y_in = (jnp.where(gy > 0, one_f, zero_f), jnp.where(gy < gyn - 1, one_f, zero_f))
    rows = lax.broadcasted_iota(jnp.int32, (NR, NW), 0)
    lanes = lax.broadcasted_iota(jnp.int32, (NR, NW), 1)
    first_z = jnp.where(col == 0, NL, NW - 4)
    row_mask = jnp.where(rows < NB, one_f, jnp.where(rows < NB + 4, y_in[1], y_in[0]))
    lane_mask = jnp.where((lanes < NL) | ((lanes >= first_z) & (lanes < first_z + 4)), one_f, zero_f)
    mask = row_mask * lane_mask
    tile_mask = lane_mask[:, NL:]
    tile_lanes = lanes[:, :128]

    def slab_in(s):
        return jnp.where(s < W, x_in[0], jnp.where(s >= W + NB, x_in[1], one_f))

    zi = lax.broadcasted_iota(jnp.int32, (NL, 128), 0)
    li = lax.broadcasted_iota(jnp.int32, (NL, 128), 1)
    place = jnp.where((li // 16 == lax.rem(gx, 8)) & (lax.rem(li, 16) == zi // AGG), one_f, zero_f)
    ki = lax.broadcasted_iota(jnp.int32, (128, NW), 0)
    ci = lax.broadcasted_iota(jnp.int32, (128, NW), 1)
    per = NL // AGG
    coarse_of = jnp.where(
        ci < NL, col * per + ci // AGG, jnp.where(col == 0, per, per - 1)
    )
    expand = jnp.where(ki == coarse_of, one_f, zero_f)

    def block_row(acc):
        return jnp.sum(dot(acc[:8] + acc[8:], place), axis=0, keepdims=True)

    started = []

    def remote(src_ref, dst_ref, send, recv, to):
        c = pltpu.make_async_remote_copy(
            src_ref=src_ref, dst_ref=dst_ref, send_sem=send, recv_sem=recv,
            device_id=to, device_id_type=MESH,
        )
        c.start()
        return c

    def gather_rows(v):
        for p in row_peers:
            remote(g1.at[v, gx], g1.at[v, gx], gsend.at[v, 0], grecv.at[v, 0], p)

    def wait_gather(ref, sem):
        pltpu.make_async_copy(ref, ref, sem).wait()

    def gather_plane(v):
        wait_gather(g1.at[v, pl.ds(0, gxn - 1)], grecv.at[v, 0])
        slot = col * gyn + gy
        for h in range(nxh):
            tot = g1[v, h * 8]
            for k in range(1, 8):
                tot = tot + g1[v, h * 8 + k]
            for kind in range(2):
                g2[v, slot, kind * nxh + h : kind * nxh + h + 1, :] = tot[kind : kind + 1]
        for p in plane_peers:
            remote(g2.at[v, slot], g2.at[v, slot], gsend.at[v, 1], grecv.at[v, 1], p)

    def unpack_plane(v, kind):
        n = gyn * nxh
        for c in range(coln):
            for y in range(gyn):
                rv[c, y * nxh : (y + 1) * nxh, :] = g2[v, c * gyn + y, kind * nxh : (kind + 1) * nxh, :]
        low, high = rv[0], rv[1]
        lane = lax.broadcasted_iota(jnp.int32, (n, 128), 1)
        out = []
        for k in range(8):
            a = pltpu.roll(low, (128 - 16 * k) % 128, 1)
            b = pltpu.roll(high, (128 + 16 - 16 * k) % 128, 1)
            out.append(jnp.where(lane < 16, a, jnp.where(lane < 32, b, zero_f)))
        return jnp.concatenate(out, axis=0)

    def send_halo(v, buf, extra):
        copies = []
        for s in range(NB):
            t = buf[W + s, 0:NB, 0:NL]
            ysend[v, 0, W * s : W * s + W, :] = t[0:W]
            ysend[v, 1, W * s : W * s + W, :] = t[NB - W : NB]
        if extra:
            for s in range(NB):
                t = q[s]
                ysend[v, 0, 48 + s : 49 + s, :] = t[0:1]
                ysend[v, 1, 48 + s : 49 + s, :] = t[NB - 1 : NB]
        ny = 64 if extra else 48
        for b in range(2):
            copies.append(remote(
                ysend.at[v, b, pl.ds(0, ny)], yrecv.at[v, 1 - b, pl.ds(0, ny)],
                hsend.at[v, b], hrecv.at[v, 1 - b], (gx, ys[b], col)))
        for a in range(2):
            s0 = W if a == 0 else NB
            d0 = W + NB if a == 0 else 0
            copies.append(remote(
                buf.at[pl.ds(s0, W), pl.ds(0, NB), pl.ds(0, NL)],
                buf.at[pl.ds(d0, W), pl.ds(0, NB), pl.ds(0, NL)],
                hsend.at[v, 2 + a], hrecv.at[v, 2 + 1 - a], (xs[a], gy, col)))
            if extra:
                s0 = W if a == 0 else W + NB - 1
                d0 = W + NB if a == 0 else W - 1
                copies.append(remote(
                    qf.at[s0, pl.ds(0, NB), pl.ds(0, NL)],
                    qf.at[d0, pl.ds(0, NB), pl.ds(0, NL)],
                    hsend.at[v, 9 + a], hrecv.at[v, 9 + 1 - a], (xs[a], gy, col)))
        for a in range(2):
            for b in range(2):
                k = a * 2 + b
                for j in range(W):
                    s = (0 if a == 0 else NB - W) + j
                    t = buf[W + s, 0:NB, 0:NL]
                    csend[v, k, 4 * j : 4 * j + W, :] = t[0:W] if b == 0 else t[NB - W : NB]
                if extra:
                    t = q[0 if a == 0 else NB - 1]
                    csend[v, k, 3:4, :] = t[0:1] if b == 0 else t[NB - 1 : NB]
                there = (1 - a) * 2 + (1 - b)
                copies.append(remote(
                    csend.at[v, k], crecv.at[v, there],
                    hsend.at[v, 4 + k], hrecv.at[v, 4 + there], (xs[a], ys[b], col)))
        started.extend(copies)
        return copies

    def take_halo(v, buf, copies, extra):
        for c in copies:
            c.wait_recv()
        for b in range(2):
            r0 = NR - W if b == 0 else NB
            qrow = NR - 1 if b == 0 else NB
            for s in range(NB):
                buf[W + s, r0 : r0 + W, 0:NL] = yrecv[v, b, W * s : W * s + W, :] * y_in[b]
                if extra:
                    qf[W + s, qrow : qrow + 1, 0:NL] = yrecv[v, b, 48 + s : 49 + s, :] * y_in[b]
            for a in range(2):
                k = a * 2 + b
                inside = x_in[a] * y_in[b]
                d0 = 0 if a == 0 else W + NB
                for j in range(W):
                    buf[d0 + j, r0 : r0 + W, 0:NL] = crecv[v, k, 4 * j : 4 * j + W, :] * inside
                if extra:
                    d0 = W - 1 if a == 0 else W + NB
                    qf[d0, qrow : qrow + 1, 0:NL] = crecv[v, k, 3:4, :] * inside
        for a in range(2):
            d0 = 0 if a == 0 else W + NB

            @pl.when(gx == (0 if a == 0 else gxn - 1))
            def _():
                buf[pl.ds(d0, W), 0:NB, 0:NL] = jnp.zeros((W, NB, NL), jnp.float32)
                if extra:
                    qf[W - 1 if a == 0 else W + NB, 0:NB, 0:NL] = jnp.zeros((NB, NL), jnp.float32)

    inner = pl.multiple_of(other * 128, 128)

    def pack_z(buf, slabs):
        acc = jnp.zeros((NR, 128), jnp.float32)
        for s in slabs:
            t = buf[s, :, pl.ds(inner, 128)]
            acc = jnp.where(tile_lanes // 4 == s, pltpu.roll(t, 4 * s + 4 * other, 1), acc)
        return acc

    def unpack_z(acc, buf, slabs):
        for s in slabs:
            t = pltpu.roll(acc, lax.rem(128 - 4 * s - 4 * col, 128), 1)
            buf[s, :, NL:NW] = jnp.where(tile_mask > 0.5, t, zero_f)

    def send_z(v, buf, extra):
        zsend[v, 0] = pack_z(buf, range(NS))
        if extra:
            zsend[v, 1] = pack_z(qf, range(W - 1, W + NB + 1))
        n = 2 if extra else 1
        c = remote(
            zsend.at[v, pl.ds(0, n)], zrecv.at[v, pl.ds(0, n)],
            hsend.at[v, 8], hrecv.at[v, 8], (gx, gy, other))
        started.append(c)
        return c

    def take_z(v, buf, copy, extra):
        copy.wait_recv()
        unpack_z(zrecv[v, 0], buf, range(NS))
        if extra:
            unpack_z(zrecv[v, 1], qf, range(W - 1, W + NB + 1))

    for v in range(VISITS):
        for s in range(NS):
            field[v, s, NB:NR, :] = jnp.zeros((NR - NB, NW), jnp.float32)
    for s in range(W - 1, W + NB + 1):
        qf[s, NB:NR, :] = jnp.zeros((NR - NB, NW), jnp.float32)

    locals_[0].wait()
    locals_[1].wait()
    rhs_acc = jnp.zeros((NB, NL), jnp.float32)
    cond_acc = jnp.zeros((NB, NL), jnp.float32)
    for s in range(NB):
        a, b = src[s], q[s]
        rhs_acc = rhs_acc + a
        cond_acc = cond_acc + b
        field[0, W + s, 0:NB, 0:NL] = a / b
        qf[W + s, 0:NB, 0:NL] = b
    cond_row = block_row(cond_acc)

    def post(v, acc):
        g1[v, gx] = jnp.concatenate([block_row(acc), cond_row], axis=0)

    post(0, rhs_acc)
    for c in locals_[2:]:
        c.wait()
    pl.semaphore_wait(barrier, len(peers))

    for v in range(VISITS):
        extra = v == 0
        last = v == VISITS - 1
        buf = field.at[v]
        gather_rows(v)
        copies = send_halo(v, buf, extra)
        gather_plane(v)
        take_halo(v, buf, copies, extra)
        zcopy = send_z(v, buf, extra)

        wait_gather(g2.at[v, pl.ds(0, gyn * coln - 1)], grecv.at[v, 1])
        if extra:
            cond = unpack_plane(v, 1)
            inv = jnp.where(
                lax.broadcasted_iota(jnp.int32, cond.shape, 1) < per * coln, cond * (1.0 / AGG**3), one_f)
            inv = one_f / inv
            qcinv[...] = inv
            qcsel[...] = dot(tab[16:32], inv)
        t = unpack_plane(v, 0) * qcinv[...]
        t = dot(vyx[...], dot(t, vz[...])) * gain[...]
        t = dot(dot(tab[0:16], t), vz[...]) * qcsel[...]
        expanded[...] = dot(t, expand)

        take_z(v, buf, zcopy, extra)

        def emit_one(s, b):
            one[s] = mask * slab_in(s) * (c1 * buf[s] + c2 * b)

        stencil(lambda s: buf[s], emit_one, 1, NS - 2, 5)

        e = expanded[...]
        for k in range(0, 9, 3):
            part[k // 3] = jnp.where(
                rows < NB, e[k + 1 : k + 2],
                jnp.where(rows < NB + 4, e[k + 2 : k + 3], e[k : k + 1]))

        def emit_two(s, b):
            k = jnp.where(s < W, 0, jnp.where(s >= W + NB, 2, 1))
            two[s] = mask * slab_in(s) * (c0 * buf[s] + b) + qf[s] * part[k]

        stencil(lambda s: one[s], emit_two, W - 1, NB + 2, 6)

        if not last:
            sums[...] = jnp.zeros((NB, NL), jnp.float32)

        def emit_three(s, b):
            own = two[s, 0:NB, 0:NL]
            i = s - W
            rem = buf[s, 0:NB, 0:NL] - (8.0 + SHIFT) * own + 0.125 * b[0:NB, 0:NL]
            tot = own if v == 0 else total[i] + own
            if last:
                sol_ref[i] = tot / q[i]
                res_ref[i] = rem * q[i]
            else:
                total[i] = tot
                field[v + 1, s, 0:NB, 0:NL] = rem
                sums[...] += rem * q[i]

        stencil(lambda s: two[s], emit_three, W, NB, 4)

        if not last:
            post(v + 1, sums[...])

    for v in range(VISITS):
        wait_gather(g1.at[v, pl.ds(0, gxn - 1)], gsend.at[v, 0])
        wait_gather(g2.at[v, pl.ds(0, gyn * coln - 1)], gsend.at[v, 1])
    for c in started:
        c.wait_send()


def local(size, consts, source, conductance):
    gxn, gyn, coln = size
    nxh = gxn // 8
    n = gxn * gyn
    f32 = jnp.float32
    block = jax.ShapeDtypeStruct((NB, NB, NL), f32)
    vmem = pltpu.VMEM
    dma = pltpu.SemaphoreType.DMA
    return pl.pallas_call(
        functools.partial(kernel, size),
        out_shape=(block, block),
        in_specs=[pl.BlockSpec(memory_space=pl.ANY)] * 6,
        out_specs=(pl.BlockSpec(memory_space=vmem),) * 2,
        scratch_shapes=[
            vmem((NB, NB, NL), f32),
            vmem((NB, NB, NL), f32),
            vmem((n, n), f32),
            vmem((128, 128), f32),
            vmem((n, 128), f32),
            vmem((32, n), f32),
            vmem((VISITS, NS, NR, NW), f32),
            vmem((NS, NR, NW), f32),
            vmem((NS, NR, NW), f32),
            vmem((NS, NR, NW), f32),
            vmem((NB, NB, NL), f32),
            vmem((16, NW), f32),
            vmem((3, NR, NW), f32),
            vmem((NB, NL), f32),
            vmem((VISITS, 2, 64, NL), f32),
            vmem((VISITS, 2, 64, NL), f32),
            vmem((VISITS, 4, 16, NL), f32),
            vmem((VISITS, 4, 16, NL), f32),
            vmem((VISITS, 2, NR, 128), f32),
            vmem((VISITS, 2, NR, 128), f32),
            vmem((VISITS, gxn, 2, 128), f32),
            vmem((VISITS, coln * gyn, 2 * nxh, 128), f32),
            vmem((coln, gyn * nxh, 128), f32),
            vmem((n, 128), f32),
            vmem((16, 128), f32),
            dma((6,)),
            dma((VISITS, 11)),
            dma((VISITS, 11)),
            dma((VISITS, 2)),
            dma((VISITS, 2)),
        ],
        compiler_params=pltpu.CompilerParams(
            collective_id=0, has_side_effects=True, vmem_limit_bytes=48 * 1024 * 1024
        ),
    )(source, conductance, *consts)


def solution(mesh):
    size = (mesh.shape["gx"], mesh.shape["gy"], mesh.shape["col"])
    consts = coarse_constants(size[0], size[1], NL // AGG * size[2])
    spec = P("gx", "gy", "col")
    return jax.shard_map(
        lambda a, b: local(size, [jnp.asarray(c) for c in consts], a, b),
        mesh=mesh,
        in_specs=(spec, spec),
        out_specs=(spec, spec),
        check_vma=False,
    )
```

```python
import functools
import math

import jax
import jax.numpy as jnp
import numpy as np
from jax import lax
from jax.experimental import pallas as pl
from jax.experimental.pallas import tpu as pltpu
from jax.sharding import PartitionSpec as P

AGG = 16
DEGREE = 3
VISITS = 3
CCYC = 4

SHIFT = 0.05
CENTER = 7.0 + SHIFT
UPPER = (8.0 + SHIFT) / CENTER
FINE_LOWER = UPPER / 4.0
COARSE_LOWER = SHIFT / CENTER
PROLONG = 0.5

NB = 16
NL = 256
W = 3
NS = NB + 2 * W
NR = 24
NW = 384
MESH = pl.DeviceIdType.MESH
HIGH = lax.Precision.HIGHEST


def cheb_poly(lower, upper):
    theta, delta = (upper + lower) / 2.0, (upper - lower) / 2.0
    sigma = theta / delta
    rho = 1.0 / sigma
    op = np.poly1d([-1.0, 8.0 + SHIFT])
    rem = np.poly1d([1.0])
    direction = rem * (1.0 / (CENTER * theta))
    total = direction
    for _ in range(DEGREE - 1):
        rem = rem - op * direction
        rho_new = 1.0 / (2.0 * sigma - rho)
        direction = (rho_new * rho) * direction + (2.0 * rho_new / delta / CENTER) * rem
        total = total + direction
        rho = rho_new
    return total


def coarse_gain(lam):
    c = cheb_poly(COARSE_LOWER, UPPER)(lam)
    err = np.zeros_like(lam)
    for _ in range(CCYC):
        err = err + c * (1.0 - (8.0 + SHIFT - lam) * err)
    return err


def sine(n):
    k = np.arange(1, n + 1)
    v = math.sqrt(2.0 / (n + 1)) * np.sin(np.pi * np.outer(k, k) / (n + 1))
    return v, 1.0 + np.cos(np.pi * k / (n + 1))


def coarse_constants(gx, gy, cz):
    vx, lx = sine(gx)
    vy, ly = sine(gy)
    vz, lz = sine(cz)
    order = [(x, y) for x in range(gx) for y in range(gy)]
    xs = np.array([o[0] for o in order])
    ys = np.array([o[1] for o in order])
    n = len(order)
    vyx = vx[np.ix_(xs, xs)] * vy[np.ix_(ys, ys)]
    lam = (lx[xs] * ly[ys])[:, None] * lz[None, :]
    gain = np.zeros((n, 128))
    gain[:, :cz] = PROLONG * AGG ** (-1.5) * coarse_gain(lam)
    vzp = np.zeros((128, 128))
    vzp[:cz, :cz] = vz
    where = {o: i for i, o in enumerate(order)}
    table = np.zeros((gx, gy, 32, n))
    for x in range(gx):
        for y in range(gy):
            for dx in range(3):
                for dy in range(3):
                    at = where.get((x + dx - 1, y + dy - 1))
                    if at is not None:
                        table[x, y, dx * 3 + dy] = vyx[at]
                        table[x, y, 16 + dx * 3 + dy, at] = 1.0
    f32 = np.float32
    return vyx.astype(f32), vzp.astype(f32), gain.astype(f32), table.reshape(gx * gy, 32, n).astype(f32)


def dot(a, b):
    return jnp.dot(a, b, precision=HIGH, preferred_element_type=jnp.float32)


def yz_sum(v):
    v = v + pltpu.roll(v, v.shape[0] - 1, 0)
    v = v + pltpu.roll(v, 1, 0)
    v = v + pltpu.roll(v, v.shape[1] - 1, 1)
    return v + pltpu.roll(v, 1, 1)


def stencil(load, emit, first, count, group):
    before = yz_sum(load(first - 1))
    here = yz_sum(load(first))

    def body(i, carry):
        pair, here = carry
        for k in range(group):
            s = first + i * group + k
            after = yz_sum(load(s + 1))
            pair_after = here + after
            emit(s, pair + pair_after)
            pair, here = pair_after, after
        return pair, here

    lax.fori_loop(0, count // group, body, (before + here, here))


def far_first(nz, ny):
    def ring(d, n):
        return min(d, n - d)

    every = [(dz, dy, dx) for dz in range(nz) for dy in range(ny) for dx in range(4)]
    hops = lambda d: ring(d[0], nz) + ring(d[1], ny) + ring(d[2], 4)
    return sorted((d for d in every if d != (0, 0, 0)), key=lambda d: (-hops(d), d))


def kernel(
    size,
    src_hbm, q_hbm, vyx_hbm, vz_hbm, gain_hbm, tab_hbm,
    tot_ref, rem_ref,
    src, q, vyx, vz, gain, tab,
    field, qf, one, two, expanded, part, sums,
    pair, coarse, qcinv, qcsel, vze,
    lsem, hsend, hrecv, gsend, grecv,
):
    gxn, gyn, coln = size
    gx, gy, col = lax.axis_index("gx"), lax.axis_index("gy"), lax.axis_index("col")
    other = 1 - col
    me = gx * gyn + gy
    poly = cheb_poly(FINE_LOWER, UPPER).coeffs
    c2, c1, c0 = (float(c) * 8.0**-k for c, k in zip(poly, (2, 1, 0)))

    local_copies = [
        pltpu.make_async_copy(a, b, lsem.at[k])
        for k, (a, b) in enumerate((
            (src_hbm, src), (q_hbm, q), (tab_hbm.at[me], tab),
            (vyx_hbm, vyx), (vz_hbm, vz), (gain_hbm, gain)))
    ]
    for c in local_copies:
        c.start()

    nz, ny = gxn // 2, gyn // 2
    z, y, x = gx // 2, gy // 2, lax.rem(gy, 2) * 2 + lax.rem(gx, 2)
    z_of = [lax.rem(z + d, nz) * 2 for d in range(nz)]
    y_of = [lax.rem(y + d, ny) * 2 for d in range(ny)]
    x_of = [lax.rem(x + d, 4) for d in range(4)]
    lo_of, hi_of = [lax.rem(a, 2) for a in x_of], [a // 2 for a in x_of]
    peers = [(z_of[dz] + lo_of[dx], y_of[dy] + hi_of[dx], col) for dz, dy, dx in far_first(nz, ny)]
    sibling = (gx, gy, other)

    barrier = pltpu.get_barrier_semaphore()
    for p in peers + [sibling]:
        pl.semaphore_signal(barrier, inc=1, device_id=p, device_id_type=MESH)

    xs = (lax.rem(gx + gxn - 1, gxn), lax.rem(gx + 1, gxn))
    ys = (lax.rem(gy + gyn - 1, gyn), lax.rem(gy + 1, gyn))

    one_f = jnp.float32(1.0)
    zero_f = jnp.float32(0.0)
    x_in = (jnp.where(gx > 0, one_f, zero_f), jnp.where(gx < gxn - 1, one_f, zero_f))
    y_in = (jnp.where(gy > 0, one_f, zero_f), jnp.where(gy < gyn - 1, one_f, zero_f))
    rows = lax.broadcasted_iota(jnp.int32, (NR, NW), 0)
    lanes = lax.broadcasted_iota(jnp.int32, (NR, NW), 1)
    first_z = jnp.where(col == 0, NL, NW - 4)
    row_mask = jnp.where(rows < NB, one_f, jnp.where(rows < NB + 4, y_in[1], y_in[0]))
    lane_mask = jnp.where((lanes < NL) | ((lanes >= first_z) & (lanes < first_z + 4)), one_f, zero_f)
    mask = row_mask * lane_mask

    def slab_in(s):
        return jnp.where(s < W, x_in[0], jnp.where(s >= W + NB, x_in[1], one_f))

    per = NL // AGG
    zi = lax.broadcasted_iota(jnp.int32, (NL, 128), 0) // AGG + col * per
    li = lax.broadcasted_iota(jnp.int32, (NL, 128), 1)
    place = jnp.where(li == zi, one_f, zero_f)
    ki = lax.broadcasted_iota(jnp.int32, (128, NW), 0)
    ci = lax.broadcasted_iota(jnp.int32, (128, NW), 1)
    coarse_of = jnp.where(
        ci < NL, col * per + ci // AGG, jnp.where(col == 0, per, per - 1)
    )
    valid = (ci < NL) | ((ci >= first_z) & (ci < first_z + 4))
    expand = jnp.where((ki == coarse_of) & valid, one_f, zero_f)

    def block_row(acc):
        return jnp.sum(dot(acc[:8] + acc[8:], place), axis=0, keepdims=True)

    started = []

    def remote(src_ref, dst_ref, send, recv, to):
        c = pltpu.make_async_remote_copy(
            src_ref=src_ref, dst_ref=dst_ref, send_sem=send, recv_sem=recv,
            device_id=to, device_id_type=MESH,
        )
        c.start()
        return c

    def send_pair(v, row):
        pair[v, 0:1, :] = row
        c = remote(pair.at[v, pl.ds(0, 1)], pair.at[v, pl.ds(8, 1)], hsend.at[v, 0], hrecv.at[v, 0], sibling)
        started.append(c)
        return c

    def gather(v, copy):
        copy.wait_recv()
        mine = coarse.at[v, pl.ds(me, 1)]
        mine[...] = pair[v, 0:1, :] + pair[v, 8:9, :]
        for p in peers:
            remote(mine, mine, gsend.at[v], grecv.at[v], p)

    def wait_rows(v, sem):
        ref = coarse.at[v, pl.ds(0, len(peers))]
        pltpu.make_async_copy(ref, ref, sem.at[v]).wait()

    def send_halo(v, buf, width, base):
        copies = []
        slabs = ((W, W + NB), (W + NB - width, W - width))
        lines = ((0, NB), (NB - width, NR - width))
        for a in (0, 1, None):
            for b in (0, 1, None):
                if a is None and b is None:
                    continue
                s0, s1, sn = (W, W, NB) if a is None else slabs[a] + (width,)
                r0, r1, rn = (0, 0, NB) if b is None else lines[b] + (width,)
                to = (gx if a is None else xs[a], gy if b is None else ys[b], col)
                code = lambda a, b: base + (2 if a is None else a) * 3 + (2 if b is None else b)
                there = code(None if a is None else 1 - a, None if b is None else 1 - b)
                copies.append(remote(
                    buf.at[pl.ds(s0, sn), pl.ds(r0, rn), pl.ds(0, NL)],
                    buf.at[pl.ds(s1, sn), pl.ds(r1, rn), pl.ds(0, NL)],
                    hsend.at[v, code(a, b)], hrecv.at[v, there], to))
        started.extend(copies)
        return copies

    inner = pl.multiple_of(other * 128, 128)

    def send_z(v, buf, boxes, base):
        copies = []
        for k, (s, sn, r, rn) in enumerate(boxes):
            copies.append(remote(
                buf.at[pl.ds(s, sn), pl.ds(r, rn), pl.ds(inner, 128)],
                buf.at[pl.ds(s, sn), pl.ds(r, rn), pl.ds(NL, 128)],
                hsend.at[v, base + k], hrecv.at[v, base + k], sibling))
        started.extend(copies)
        return copies

    own_box = [(W, NB, 0, NB)]

    def outer_boxes(width):
        return [(W, NB, NB, NR - NB), (W - width, width, 0, NR), (W + NB, width, 0, NR)]

    local_copies[0].wait()
    local_copies[1].wait()
    rhs_acc = jnp.zeros((NB, NL), jnp.float32)
    cond_acc = jnp.zeros((NB, NL), jnp.float32)
    for s in range(NB):
        rhs_acc = rhs_acc + src[s]
        cond_acc = cond_acc + q[s]
    row = block_row(rhs_acc) + pltpu.roll(block_row(cond_acc), 32, 1)
    for s in range(NB):
        field[0, W + s, 0:NB, 0:NL] = src[s] / q[s]
        qf[W + s, 0:NB, 0:NL] = q[s]
    for c in local_copies[2:]:
        c.wait()
    vze[...] = dot(vz[...], expand)
    pl.semaphore_wait(barrier, len(peers) + 1)

    for v in range(VISITS):
        extra = v == 0
        last = v == VISITS - 1
        buf = field.at[v]
        paired = send_pair(v, row)
        copies = send_halo(v, buf, W, 1)
        near = send_z(v, buf, own_box, 10)
        if extra:
            copies += send_halo(v, qf, 1, 14)
            near += send_z(v, qf, own_box, 23)
        gather(v, paired)
        for c in copies:
            c.wait_recv()
        near += send_z(v, buf, outer_boxes(W), 11)
        if extra:
            near += send_z(v, qf, outer_boxes(1), 24)
        wait_rows(v, grecv)
        t = coarse[v]
        if extra:
            lane = lax.broadcasted_iota(jnp.int32, t.shape, 1)
            cond = pltpu.roll(t, 96, 1) * (1.0 / AGG**3)
            inv = one_f / jnp.where(lane < per * coln, cond, one_f)
            qcinv[...] = inv
            qcsel[...] = dot(dot(tab[16:32], inv), expand)
        t = dot(vyx[...], dot(t * qcinv[...], vz[...])) * gain[...]
        expanded[...] = dot(dot(tab[0:16], t), vze[...]) * qcsel[...]
        e = expanded[...]
        for k in range(0, 9, 3):
            part[k // 3] = jnp.where(
                rows < NB, e[k + 1 : k + 2],
                jnp.where(rows < NB + 4, e[k + 2 : k + 3], e[k : k + 1]))

        for c in near:
            c.wait_recv()

        def emit_one(s, b):
            one[s] = mask * slab_in(s) * (c1 * buf[s] + c2 * b)

        stencil(lambda s: mask * slab_in(s) * buf[s], emit_one, 1, NS - 2, 5)

        def emit_two(s, b):
            k = jnp.where(s < W, 0, jnp.where(s >= W + NB, 2, 1))
            two[s] = mask * slab_in(s) * (c0 * buf[s] + b) + qf[s] * part[k]

        stencil(lambda s: one[s], emit_two, W - 1, NB + 2, 6)

        if not last:
            sums[...] = jnp.zeros((NB, NL), jnp.float32)

        def emit_three(s, b):
            own = two[s, 0:NB, 0:NL]
            i = s - W
            rem = buf[s, 0:NB, 0:NL] - (8.0 + SHIFT) * own + 0.125 * b[0:NB, 0:NL]
            tot_ref[i] = own if v == 0 else tot_ref[i] + own
            if last:
                rem_ref[i] = rem
            else:
                field[v + 1, s, 0:NB, 0:NL] = rem
                sums[...] += rem * q[i]

        stencil(lambda s: two[s], emit_three, W, NB, 4)

        if not last:
            row = block_row(sums[...])

    for v in range(VISITS):
        wait_rows(v, gsend)
    for c in started:
        c.wait_send()


def local(size, consts, source, conductance):
    gxn, gyn, coln = size
    n = gxn * gyn
    f32 = jnp.float32
    block = jax.ShapeDtypeStruct((NB, NB, NL), f32)
    vmem = pltpu.VMEM
    dma = pltpu.SemaphoreType.DMA
    total, remainder = pl.pallas_call(
        functools.partial(kernel, size),
        out_shape=(block, block),
        in_specs=[pl.BlockSpec(memory_space=pl.ANY)] * 6,
        out_specs=(pl.BlockSpec(memory_space=vmem),) * 2,
        scratch_shapes=[
            vmem((NB, NB, NL), f32),
            vmem((NB, NB, NL), f32),
            vmem((n, n), f32),
            vmem((128, 128), f32),
            vmem((n, 128), f32),
            vmem((32, n), f32),
            vmem((VISITS, NS, NR, NW), f32),
            vmem((NS, NR, NW), f32),
            vmem((NS, NR, NW), f32),
            vmem((NS, NR, NW), f32),
            vmem((16, NW), f32),
            vmem((3, NR, NW), f32),
            vmem((NB, NL), f32),
            vmem((VISITS, 16, 128), f32),
            vmem((VISITS, n, 128), f32),
            vmem((n, 128), f32),
            vmem((16, NW), f32),
            vmem((128, NW), f32),
            dma((6,)),
            dma((VISITS, 27)),
            dma((VISITS, 27)),
            dma((VISITS,)),
            dma((VISITS,)),
        ],
        compiler_params=pltpu.CompilerParams(
            collective_id=0, has_side_effects=True, vmem_limit_bytes=60 * 1024 * 1024
        ),
    )(source, conductance, *consts)
    return total / conductance, remainder * conductance


def solution(mesh):
    size = (mesh.shape["gx"], mesh.shape["gy"], mesh.shape["col"])
    consts = coarse_constants(size[0], size[1], NL // AGG * size[2])
    spec = P("gx", "gy", "col")
    return jax.shard_map(
        lambda a, b: local(size, [jnp.asarray(c) for c in consts], a, b),
        mesh=mesh,
        in_specs=(spec, spec),
        out_specs=(spec, spec),
        check_vma=False,
    )
```

```python
import functools
import math

import jax
import jax.numpy as jnp
import numpy as np
from jax import lax
from jax.experimental import pallas as pl
from jax.experimental.pallas import tpu as pltpu
from jax.sharding import PartitionSpec as P

AGG = 16
DEGREE = 3
VISITS = 3
CCYC = 4

SHIFT = 0.05
CENTER = 7.0 + SHIFT
UPPER = (8.0 + SHIFT) / CENTER
FINE_LOWER = UPPER / 4.0
COARSE_LOWER = SHIFT / CENTER
PROLONG = 0.5

NB = 16
NL = 256
W = 3
NS = NB + 2 * W
NR = 24
NW = 384
MESH = pl.DeviceIdType.MESH
G1, G2, G3 = 10, 9, 8
HALO_ORDER = ((None, 0), (None, 1), (0, 0), (0, 1), (1, 0), (1, 1), (0, None), (1, None))
HIGH = lax.Precision.HIGHEST


def cheb_poly(lower, upper):
    theta, delta = (upper + lower) / 2.0, (upper - lower) / 2.0
    sigma = theta / delta
    rho = 1.0 / sigma
    op = np.poly1d([-1.0, 8.0 + SHIFT])
    rem = np.poly1d([1.0])
    direction = rem * (1.0 / (CENTER * theta))
    total = direction
    for _ in range(DEGREE - 1):
        rem = rem - op * direction
        rho_new = 1.0 / (2.0 * sigma - rho)
        direction = (rho_new * rho) * direction + (2.0 * rho_new / delta / CENTER) * rem
        total = total + direction
        rho = rho_new
    return total


def coarse_gain(lam):
    c = cheb_poly(COARSE_LOWER, UPPER)(lam)
    err = np.zeros_like(lam)
    for _ in range(CCYC):
        err = err + c * (1.0 - (8.0 + SHIFT - lam) * err)
    return err


def sine(n):
    k = np.arange(1, n + 1)
    v = math.sqrt(2.0 / (n + 1)) * np.sin(np.pi * np.outer(k, k) / (n + 1))
    return v, 1.0 + np.cos(np.pi * k / (n + 1))


def coarse_constants(gx, gy, cz):
    vx, lx = sine(gx)
    vy, ly = sine(gy)
    vz, lz = sine(cz)
    order = [(x, y) for x in range(gx) for y in range(gy)]
    xs = np.array([o[0] for o in order])
    ys = np.array([o[1] for o in order])
    n = len(order)
    vyx = vx[np.ix_(xs, xs)] * vy[np.ix_(ys, ys)]
    lam = (lx[xs] * ly[ys])[:, None] * lz[None, :]
    gain = np.zeros((n, 128))
    gain[:, :cz] = PROLONG * AGG ** (-1.5) * coarse_gain(lam)
    vzp = np.zeros((128, 128))
    vzp[:cz, :cz] = vz
    where = {o: i for i, o in enumerate(order)}
    table = np.zeros((gx, gy, 32, n))
    for x in range(gx):
        for y in range(gy):
            for dx in range(3):
                for dy in range(3):
                    at = where.get((x + dx - 1, y + dy - 1))
                    if at is not None:
                        table[x, y, dx * 3 + dy] = vyx[at]
                        table[x, y, 16 + dx * 3 + dy, at] = 1.0
    f32 = np.float32
    return vyx.astype(f32), vzp.astype(f32), gain.astype(f32), table.reshape(gx * gy, 32, n).astype(f32)


def dot(a, b):
    return jnp.dot(a, b, precision=HIGH, preferred_element_type=jnp.float32)


def yz_sum(v):
    v = v + pltpu.roll(v, v.shape[0] - 1, 0)
    v = v + pltpu.roll(v, 1, 0)
    v = v + pltpu.roll(v, v.shape[1] - 1, 1)
    return v + pltpu.roll(v, 1, 1)


def stencil(load, emit, first, count, group):
    here = load(first)

    def body(i, carry):
        pair, here = carry
        for k in range(group):
            s = first + i * group + k
            after = load(s + 1)
            pair_after = here + after
            emit(s, yz_sum(pair + pair_after))
            pair, here = pair_after, after
        return pair, here

    carry = (load(first - 1) + here, here)
    if group == count:
        body(0, carry)
    else:
        lax.fori_loop(0, count // group, body, carry)


def far_first(ny):
    def ring(d, n):
        return min(d, n - d)

    every = [(dy, dx) for dy in range(ny) for dx in range(4)]
    return sorted(every, key=lambda d: (-ring(d[0], ny) - ring(d[1], 4), d))


def kernel(
    size,
    src_hbm, q_hbm, vyx_hbm, vz_hbm, gain_hbm, tab_hbm,
    tot_ref, rem_ref,
    src, q, vyx, vz, gain, tab,
    field, qf, one, two, expanded, part, sums,
    pair, coarse, qcinv, qcsel, vze,
    lsem, hsend, hrecv, gsend, grecv,
):
    gxn, gyn, coln = size
    gx, gy, col = lax.axis_index("gx"), lax.axis_index("gy"), lax.axis_index("col")
    other = 1 - col
    me = gx * gyn + gy
    poly = cheb_poly(FINE_LOWER, UPPER).coeffs
    c2, c1, c0 = (float(c) * 8.0**-k for c, k in zip(poly, (2, 1, 0)))

    local_copies = [
        pltpu.make_async_copy(a, b, lsem.at[k])
        for k, (a, b) in enumerate((
            (src_hbm, src), (q_hbm, q), (tab_hbm.at[me], tab),
            (vyx_hbm, vyx), (vz_hbm, vz), (gain_hbm, gain)))
    ]
    for c in local_copies:
        c.start()

    nz, ny = gxn // 2, gyn // 2
    z, y, x = gx // 2, gy // 2, lax.rem(gy, 2) * 2 + lax.rem(gx, 2)
    y_of = [lax.rem(y + d, ny) * 2 for d in range(ny)]
    x_of = [lax.rem(x + d, 4) for d in range(4)]
    lo_of, hi_of = [lax.rem(a, 2) for a in x_of], [a // 2 for a in x_of]
    plane = far_first(ny)
    n_peers = nz * ny * 4 - 1

    def each_peer(act):
        def planes(k, carry):
            dz = nz // 2 + jnp.where(lax.rem(k, 2) == 0, k // 2, -((k + 1) // 2))
            z_of = lax.rem(z + dz, nz) * 2
            for dy, dx in plane:
                act((z_of + lo_of[dx], y_of[dy] + hi_of[dx], col))
            return carry

        lax.fori_loop(0, nz - 1, planes, 0)
        for dy, dx in plane:
            if dy or dx:
                act((z * 2 + lo_of[dx], y_of[dy] + hi_of[dx], col))

    sibling = (gx, gy, other)

    barrier = pltpu.get_barrier_semaphore()

    def greet(p):
        pl.semaphore_signal(barrier, inc=1, device_id=p, device_id_type=MESH)

    each_peer(greet)
    greet(sibling)

    xs = (lax.rem(gx + gxn - 1, gxn), lax.rem(gx + 1, gxn))
    ys = (lax.rem(gy + gyn - 1, gyn), lax.rem(gy + 1, gyn))

    one_f = jnp.float32(1.0)
    zero_f = jnp.float32(0.0)
    x_in = (jnp.where(gx > 0, one_f, zero_f), jnp.where(gx < gxn - 1, one_f, zero_f))
    y_in = (jnp.where(gy > 0, one_f, zero_f), jnp.where(gy < gyn - 1, one_f, zero_f))
    rows = lax.broadcasted_iota(jnp.int32, (NR, NW), 0)
    lanes = lax.broadcasted_iota(jnp.int32, (NR, NW), 1)
    first_z = jnp.where(col == 0, NL, NW - 4)
    row_mask = jnp.where(rows < NB, one_f, jnp.where(rows < NB + 4, y_in[1], y_in[0]))
    lane_mask = jnp.where((lanes < NL) | ((lanes >= first_z) & (lanes < first_z + 4)), one_f, zero_f)
    mask = row_mask * lane_mask

    def slab_in(s):
        return jnp.where(s < W, x_in[0], jnp.where(s >= W + NB, x_in[1], one_f))

    per = NL // AGG
    zi = lax.broadcasted_iota(jnp.int32, (NL, 128), 0) // AGG + col * per
    li = lax.broadcasted_iota(jnp.int32, (NL, 128), 1)
    place = jnp.where(li == zi, one_f, zero_f)
    ki = lax.broadcasted_iota(jnp.int32, (128, NW), 0)
    ci = lax.broadcasted_iota(jnp.int32, (128, NW), 1)
    coarse_of = jnp.where(
        ci < NL, col * per + ci // AGG, jnp.where(col == 0, per, per - 1)
    )
    valid = (ci < NL) | ((ci >= first_z) & (ci < first_z + 4))
    expand = jnp.where((ki == coarse_of) & valid, one_f, zero_f)

    def block_row(acc):
        return jnp.sum(dot(acc[:8] + acc[8:], place), axis=0, keepdims=True)

    def remote(src_ref, dst_ref, send, recv, to):
        return pltpu.make_async_remote_copy(
            src_ref=src_ref, dst_ref=dst_ref, send_sem=send, recv_sem=recv,
            device_id=to, device_id_type=MESH,
        )

    def start(copies):
        for c in copies:
            c.start()

    def received(copies):
        for c in copies:
            c.wait_recv()

    def sent(copies):
        for c in copies:
            c.wait_send()

    def pair_copy(v):
        return remote(pair.at[v, pl.ds(0, 1)], pair.at[v, pl.ds(8, 1)], hsend.at[v, 0], hrecv.at[v, 0], sibling)

    def gather(v):
        mine = coarse.at[v, pl.ds(me, 1)]
        mine[...] = pair[v, 0:1, :] + pair[v, 8:9, :]
        each_peer(lambda p: remote(mine, mine, gsend.at[v], grecv.at[v], p).start())

    def wait_rows(v, sem):
        ref = coarse.at[v, pl.ds(0, n_peers)]
        pltpu.make_async_copy(ref, ref, sem.at[v]).wait()

    def halo_copies(v, buf, width, base):
        copies = []
        slabs = ((W, W + NB), (W + NB - width, W - width))
        lines = ((0, NB), (NB - width, NR - width))
        for a, b in HALO_ORDER:
            s0, s1, sn = (W, W, NB) if a is None else slabs[a] + (width,)
            r0, r1, rn = (0, 0, NB) if b is None else lines[b] + (width,)
            to = (gx if a is None else xs[a], gy if b is None else ys[b], col)
            code = lambda a, b: base + (2 if a is None else a) * 3 + (2 if b is None else b)
            there = code(None if a is None else 1 - a, None if b is None else 1 - b)
            copies.append(remote(
                buf.at[pl.ds(s0, sn), pl.ds(r0, rn), pl.ds(0, NL)],
                buf.at[pl.ds(s1, sn), pl.ds(r1, rn), pl.ds(0, NL)],
                hsend.at[v, code(a, b)], hrecv.at[v, there], to))
        return copies

    inner = pl.multiple_of(other * 128, 128)

    def z_copies(v, buf, boxes, base):
        copies = []
        for k, (s, sn, r, rn) in enumerate(boxes):
            copies.append(remote(
                buf.at[pl.ds(s, sn), pl.ds(r, rn), pl.ds(inner, 128)],
                buf.at[pl.ds(s, sn), pl.ds(r, rn), pl.ds(NL, 128)],
                hsend.at[v, base + k], hrecv.at[v, base + k], sibling))
        return copies

    own_box = [(W, NB, 0, NB)]

    def outer_boxes(width):
        return [(W, NB, NB, NR - NB), (W - width, width, 0, NR), (W + NB, width, 0, NR)]

    local_copies[0].wait()
    local_copies[1].wait()
    rhs_acc = jnp.zeros((NB, NL), jnp.float32)
    cond_acc = jnp.zeros((NB, NL), jnp.float32)
    for s in range(NB):
        rhs_acc = rhs_acc + src[s]
        cond_acc = cond_acc + q[s]
    pair[0, 0:1, :] = block_row(rhs_acc) + pltpu.roll(block_row(cond_acc), 32, 1)
    for s in range(NB):
        field[0, W + s, 0:NB, 0:NL] = src[s] / q[s]
        qf[W + s, 0:NB, 0:NL] = q[s]
        tot_ref[s] = jnp.zeros((NB, NL), jnp.float32)
    for c in local_copies[2:]:
        c.wait()
    vze[...] = dot(vz[...], expand)
    pl.semaphore_wait(barrier, n_peers + 1)

    def visit(v, carry):
        first = v == 0
        buf = field.at[v]
        paired = pair_copy(v)
        halo = halo_copies(v, buf, W, 1)
        near = z_copies(v, buf, own_box, 10)
        far = z_copies(v, buf, outer_boxes(W), 11)

        def q_halo():
            return halo_copies(v, qf, 1, 14)

        def q_near():
            return z_copies(v, qf, own_box, 23)

        def q_far():
            return z_copies(v, qf, outer_boxes(1), 24)

        start([paired] + halo + near)

        @pl.when(first)
        def _():
            start(q_halo() + q_near())

        received([paired])
        gather(v)
        received(halo)
        start(far)

        @pl.when(first)
        def _():
            received(q_halo())
            start(q_far())

        wait_rows(v, grecv)
        @pl.when(first)
        def _():
            lane = lax.broadcasted_iota(jnp.int32, (gxn * gyn, 128), 1)
            cond = pltpu.roll(coarse[v], 96, 1) * (1.0 / AGG**3)
            inv = one_f / jnp.where(lane < per * coln, cond, one_f)
            qcinv[...] = inv
            qcsel[...] = dot(dot(tab[16:32], inv), expand)
        t = dot(vyx[...], dot(coarse[v] * qcinv[...], vz[...])) * gain[...]
        expanded[...] = dot(dot(tab[0:16], t), vze[...]) * qcsel[...]
        e = expanded[...]
        for k in range(0, 9, 3):
            part[k // 3] = jnp.where(
                rows < NB, e[k + 1 : k + 2],
                jnp.where(rows < NB + 4, e[k + 2 : k + 3], e[k : k + 1]))

        received(near + far)

        def emit_one(s, b):
            one[s] = mask * slab_in(s) * (c1 * buf[s] + c2 * b)

        stencil(lambda s: mask * slab_in(s) * buf[s], emit_one, 1, NS - 2, G1)

        def emit_two(s, b):
            k = jnp.where(s < W, 0, jnp.where(s >= W + NB, 2, 1))
            two[s] = mask * slab_in(s) * (c0 * buf[s] + b) + qf[s] * part[k]

        @pl.when(first)
        def _():
            received(q_near() + q_far())

        stencil(lambda s: one[s], emit_two, W - 1, NB + 2, G2)

        sums[...] = jnp.zeros((NB, NL), jnp.float32)

        def emit_three(s, b):
            own = two[s, 0:NB, 0:NL]
            i = s - W
            rem = buf[s, 0:NB, 0:NL] - (8.0 + SHIFT) * own + 0.125 * b[0:NB, 0:NL]
            tot_ref[i] += own
            rem_ref[i] = rem
            field[v + 1, s, 0:NB, 0:NL] = rem
            sums[...] += rem * q[i]

        stencil(lambda s: two[s], emit_three, W, NB, G3)

        @pl.when(v < VISITS - 1)
        def _():
            pair[v + 1, 0:1, :] = block_row(sums[...])

        sent([paired] + halo + near + far)
        wait_rows(v, gsend)

        @pl.when(first)
        def _():
            sent(q_halo() + q_near() + q_far())

        return carry

    lax.fori_loop(0, VISITS, visit, 0)


def local(size, consts, source, conductance):
    gxn, gyn, coln = size
    n = gxn * gyn
    f32 = jnp.float32
    vmem = pltpu.VMEM
    dma = pltpu.SemaphoreType.DMA
    total, remainder = pl.pallas_call(
        functools.partial(kernel, size),
        out_shape=(vmem((NB, NB, NL), f32),) * 2,
        in_specs=[pl.BlockSpec(memory_space=pl.ANY)] * 6,
        out_specs=(pl.BlockSpec(memory_space=vmem),) * 2,
        scratch_shapes=[
            vmem((NB, NB, NL), f32),
            vmem((NB, NB, NL), f32),
            vmem((n, n), f32),
            vmem((128, 128), f32),
            vmem((n, 128), f32),
            vmem((32, n), f32),
            vmem((VISITS + 1, NS, NR, NW), f32),
            vmem((NS, NR, NW), f32),
            vmem((NS, NR, NW), f32),
            vmem((NS, NR, NW), f32),
            vmem((16, NW), f32),
            vmem((3, NR, NW), f32),
            vmem((NB, NL), f32),
            vmem((VISITS, 16, 128), f32),
            vmem((VISITS, n, 128), f32),
            vmem((n, 128), f32),
            vmem((16, NW), f32),
            vmem((128, NW), f32),
            dma((6,)),
            dma((VISITS, 27)),
            dma((VISITS, 27)),
            dma((VISITS,)),
            dma((VISITS,)),
        ],
        compiler_params=pltpu.CompilerParams(
            collective_id=0, has_side_effects=True, vmem_limit_bytes=60 * 1024 * 1024
        ),
    )(source, conductance, *consts)
    return total / conductance, remainder * conductance


def solution(mesh):
    size = (mesh.shape["gx"], mesh.shape["gy"], mesh.shape["col"])
    consts = coarse_constants(size[0], size[1], NL // AGG * size[2])
    spec = P("gx", "gy", "col")
    return jax.shard_map(
        lambda a, b: local(size, [jnp.asarray(c) for c in consts], a, b),
        mesh=mesh,
        in_specs=(spec, spec),
        out_specs=(spec, spec),
        check_vma=False,
    )
```

```python
import functools
import math

import jax
import jax.numpy as jnp
import numpy as np
from jax import lax
from jax.experimental import pallas as pl
from jax.experimental.pallas import tpu as pltpu
from jax.sharding import PartitionSpec as P

AGG = 16
DEGREE = 3
VISITS = 3
CCYC = 4

SHIFT = 0.05
CENTER = 7.0 + SHIFT
UPPER = (8.0 + SHIFT) / CENTER
FINE_LOWER = UPPER / 4.0
COARSE_LOWER = SHIFT / CENTER
PROLONG = 0.5

NB = 16
NL = 256
W = 3
NS = NB + 2 * W
NR = 24
NW = 384
MESH = pl.DeviceIdType.MESH
G1, G2, G3 = 20, 18, 16
HALO_ORDER = ((None, 0), (None, 1), (0, 0), (0, 1), (1, 0), (1, 1), (0, None), (1, None))
HIGH = lax.Precision.HIGHEST


def cheb_poly(lower, upper):
    theta, delta = (upper + lower) / 2.0, (upper - lower) / 2.0
    sigma = theta / delta
    rho = 1.0 / sigma
    op = np.poly1d([-1.0, 8.0 + SHIFT])
    rem = np.poly1d([1.0])
    direction = rem * (1.0 / (CENTER * theta))
    total = direction
    for _ in range(DEGREE - 1):
        rem = rem - op * direction
        rho_new = 1.0 / (2.0 * sigma - rho)
        direction = (rho_new * rho) * direction + (2.0 * rho_new / delta / CENTER) * rem
        total = total + direction
        rho = rho_new
    return total


def coarse_gain(lam):
    c = cheb_poly(COARSE_LOWER, UPPER)(lam)
    err = np.zeros_like(lam)
    for _ in range(CCYC):
        err = err + c * (1.0 - (8.0 + SHIFT - lam) * err)
    return err


def sine(n):
    k = np.arange(1, n + 1)
    v = math.sqrt(2.0 / (n + 1)) * np.sin(np.pi * np.outer(k, k) / (n + 1))
    return v, 1.0 + np.cos(np.pi * k / (n + 1))


def coarse_constants(gx, gy, cz):
    vx, lx = sine(gx)
    vy, ly = sine(gy)
    vz, lz = sine(cz)
    order = [(x, y) for x in range(gx) for y in range(gy)]
    xs = np.array([o[0] for o in order])
    ys = np.array([o[1] for o in order])
    n = len(order)
    vyx = vx[np.ix_(xs, xs)] * vy[np.ix_(ys, ys)]
    lam = (lx[xs] * ly[ys])[:, None] * lz[None, :]
    gain = np.zeros((n, 128))
    gain[:, :cz] = PROLONG * AGG ** (-1.5) * coarse_gain(lam)
    vzp = np.zeros((128, 128))
    vzp[:cz, :cz] = vz
    where = {o: i for i, o in enumerate(order)}
    table = np.zeros((gx, gy, 32, n))
    for x in range(gx):
        for y in range(gy):
            for dx in range(3):
                for dy in range(3):
                    at = where.get((x + dx - 1, y + dy - 1))
                    if at is not None:
                        table[x, y, dx * 3 + dy] = vyx[at]
                        table[x, y, 16 + dx * 3 + dy, at] = 1.0
    f32 = np.float32
    return vyx.astype(f32), vzp.astype(f32), gain.astype(f32), table.reshape(gx * gy, 32, n).astype(f32)


def dot(a, b):
    return jnp.dot(a, b, precision=HIGH, preferred_element_type=jnp.float32)


def y_sum(v):
    v = v + pltpu.roll(v, v.shape[0] - 1, 0)
    return v + pltpu.roll(v, 1, 0)


def z_matrix():
    i = lax.broadcasted_iota(jnp.int32, (NW, NW), 0)
    j = lax.broadcasted_iota(jnp.int32, (NW, NW), 1)
    d = jnp.abs(i - j)
    return jnp.where(d == 0, 2.0, jnp.where((d == 1) | (d == NW - 1), 1.0, 0.0)).astype(jnp.bfloat16)


def z_sum(v, tz):
    high = v.astype(jnp.bfloat16)
    low = (v - high.astype(jnp.float32)).astype(jnp.bfloat16)
    return jnp.dot(jnp.concatenate([high, low], axis=1), tz, preferred_element_type=jnp.float32)


def stencil(load, emit, tz, first, count, group, rows=NR):
    here = load(first)

    def body(i, carry):
        pair, here = carry
        out = []
        for k in range(group):
            after = load(first + i * group + k + 1)
            pair_after = here + after
            out.append(y_sum(pair + pair_after)[:rows])
            pair, here = pair_after, after
        out = z_sum(jnp.concatenate(out, axis=0), tz)
        for k in range(group):
            emit(first + i * group + k, out[k * rows : (k + 1) * rows])
        return pair, here

    carry = (load(first - 1) + here, here)
    if group == count:
        body(0, carry)
    else:
        lax.fori_loop(0, count // group, body, carry)


def far_first(ny):
    def ring(d, n):
        return min(d, n - d)

    every = [(dy, dx) for dy in range(ny) for dx in range(4)]
    return sorted(every, key=lambda d: (-ring(d[0], ny) - ring(d[1], 4), d))


def kernel(
    size,
    src_hbm, q_hbm, vyx_hbm, vz_hbm, gain_hbm, tab_hbm,
    tot_ref, rem_ref,
    src, q, vyx, vz, gain, tab,
    field, qf, one, two, expanded, part, sums,
    pair, coarse, qcinv, qcsel, vze, tz,
    lsem, hsend, hrecv, gsend, grecv,
):
    gxn, gyn, coln = size
    gx, gy, col = lax.axis_index("gx"), lax.axis_index("gy"), lax.axis_index("col")
    other = 1 - col
    me = gx * gyn + gy
    poly = cheb_poly(FINE_LOWER, UPPER).coeffs
    c2, c1, c0 = (float(c) * 8.0**-k for c, k in zip(poly, (2, 1, 0)))

    local_copies = [
        pltpu.make_async_copy(a, b, lsem.at[k])
        for k, (a, b) in enumerate((
            (src_hbm, src), (q_hbm, q), (tab_hbm.at[me], tab),
            (vyx_hbm, vyx), (vz_hbm, vz), (gain_hbm, gain)))
    ]
    for c in local_copies:
        c.start()

    nz, ny = gxn // 2, gyn // 2
    z, y, x = gx // 2, gy // 2, lax.rem(gy, 2) * 2 + lax.rem(gx, 2)
    y_of = [lax.rem(y + d, ny) * 2 for d in range(ny)]
    x_of = [lax.rem(x + d, 4) for d in range(4)]
    lo_of, hi_of = [lax.rem(a, 2) for a in x_of], [a // 2 for a in x_of]
    plane = far_first(ny)
    n_peers = nz * ny * 4 - 1

    def each_peer(act):
        def planes(k, carry):
            dz = nz // 2 + jnp.where(lax.rem(k, 2) == 0, k // 2, -((k + 1) // 2))
            z_of = lax.rem(z + dz, nz) * 2
            for dy, dx in plane:
                act((z_of + lo_of[dx], y_of[dy] + hi_of[dx], col))
            return carry

        lax.fori_loop(0, nz - 1, planes, 0)
        for dy, dx in plane:
            if dy or dx:
                act((z * 2 + lo_of[dx], y_of[dy] + hi_of[dx], col))

    sibling = (gx, gy, other)

    barrier = pltpu.get_barrier_semaphore()

    def greet(p):
        pl.semaphore_signal(barrier, inc=1, device_id=p, device_id_type=MESH)

    each_peer(greet)
    greet(sibling)

    xs = (lax.rem(gx + gxn - 1, gxn), lax.rem(gx + 1, gxn))
    ys = (lax.rem(gy + gyn - 1, gyn), lax.rem(gy + 1, gyn))

    one_f = jnp.float32(1.0)
    zero_f = jnp.float32(0.0)
    x_in = (jnp.where(gx > 0, one_f, zero_f), jnp.where(gx < gxn - 1, one_f, zero_f))
    y_in = (jnp.where(gy > 0, one_f, zero_f), jnp.where(gy < gyn - 1, one_f, zero_f))
    rows = lax.broadcasted_iota(jnp.int32, (NR, NW), 0)
    lanes = lax.broadcasted_iota(jnp.int32, (NR, NW), 1)
    first_z = jnp.where(col == 0, NL, NW - 4)
    row_mask = jnp.where(rows < NB, one_f, jnp.where(rows < NB + 4, y_in[1], y_in[0]))
    lane_mask = jnp.where((lanes < NL) | ((lanes >= first_z) & (lanes < first_z + 4)), one_f, zero_f)
    mask = row_mask * lane_mask

    def slab_in(s):
        return jnp.where(s < W, x_in[0], jnp.where(s >= W + NB, x_in[1], one_f))

    per = NL // AGG
    zi = lax.broadcasted_iota(jnp.int32, (NL, 128), 0) // AGG + col * per
    li = lax.broadcasted_iota(jnp.int32, (NL, 128), 1)
    place = jnp.where(li == zi, one_f, zero_f)
    ki = lax.broadcasted_iota(jnp.int32, (128, NW), 0)
    ci = lax.broadcasted_iota(jnp.int32, (128, NW), 1)
    coarse_of = jnp.where(
        ci < NL, col * per + ci // AGG, jnp.where(col == 0, per, per - 1)
    )
    valid = (ci < NL) | ((ci >= first_z) & (ci < first_z + 4))
    expand = jnp.where((ki == coarse_of) & valid, one_f, zero_f)

    def block_row(acc):
        return jnp.sum(dot(acc[:8] + acc[8:], place), axis=0, keepdims=True)

    def remote(src_ref, dst_ref, send, recv, to):
        return pltpu.make_async_remote_copy(
            src_ref=src_ref, dst_ref=dst_ref, send_sem=send, recv_sem=recv,
            device_id=to, device_id_type=MESH,
        )

    def start(copies):
        for c in copies:
            c.start()

    def received(copies):
        for c in copies:
            c.wait_recv()

    def sent(copies):
        for c in copies:
            c.wait_send()

    def pair_copy(v):
        return remote(pair.at[v, pl.ds(0, 1)], pair.at[v, pl.ds(8, 1)], hsend.at[v, 0], hrecv.at[v, 0], sibling)

    def gather(v):
        mine = coarse.at[v, pl.ds(me, 1)]
        mine[...] = pair[v, 0:1, :] + pair[v, 8:9, :]
        each_peer(lambda p: remote(mine, mine, gsend.at[v], grecv.at[v], p).start())

    def wait_rows(v, sem):
        ref = coarse.at[v, pl.ds(0, n_peers)]
        pltpu.make_async_copy(ref, ref, sem.at[v]).wait()

    def halo_copies(v, buf, width, base):
        copies = []
        slabs = ((W, W + NB), (W + NB - width, W - width))
        lines = ((0, NB), (NB - width, NR - width))
        for a, b in HALO_ORDER:
            s0, s1, sn = (W, W, NB) if a is None else slabs[a] + (width,)
            r0, r1, rn = (0, 0, NB) if b is None else lines[b] + (width,)
            to = (gx if a is None else xs[a], gy if b is None else ys[b], col)
            code = lambda a, b: base + (2 if a is None else a) * 3 + (2 if b is None else b)
            there = code(None if a is None else 1 - a, None if b is None else 1 - b)
            copies.append(remote(
                buf.at[pl.ds(s0, sn), pl.ds(r0, rn), pl.ds(0, NL)],
                buf.at[pl.ds(s1, sn), pl.ds(r1, rn), pl.ds(0, NL)],
                hsend.at[v, code(a, b)], hrecv.at[v, there], to))
        return copies

    inner = pl.multiple_of(other * 128, 128)

    def z_copies(v, buf, boxes, base):
        copies = []
        for k, (s, sn, r, rn) in enumerate(boxes):
            copies.append(remote(
                buf.at[pl.ds(s, sn), pl.ds(r, rn), pl.ds(inner, 128)],
                buf.at[pl.ds(s, sn), pl.ds(r, rn), pl.ds(NL, 128)],
                hsend.at[v, base + k], hrecv.at[v, base + k], sibling))
        return copies

    own_box = [(W, NB, 0, NB)]

    def outer_boxes(width):
        return [(W, NB, NB, NR - NB), (W - width, width, 0, NR), (W + NB, width, 0, NR)]

    local_copies[0].wait()
    local_copies[1].wait()
    rhs_acc = jnp.zeros((NB, NL), jnp.float32)
    cond_acc = jnp.zeros((NB, NL), jnp.float32)
    for s in range(NB):
        rhs_acc = rhs_acc + src[s]
        cond_acc = cond_acc + q[s]
    pair[0, 0:1, :] = block_row(rhs_acc) + pltpu.roll(block_row(cond_acc), 32, 1)
    for s in range(NB):
        field[0, W + s, 0:NB, 0:NL] = src[s] / q[s]
        qf[W + s, 0:NB, 0:NL] = q[s]
        tot_ref[s] = jnp.zeros((NB, NL), jnp.float32)
    for c in local_copies[2:]:
        c.wait()
    vze[...] = dot(vz[...], expand)
    t = z_matrix()
    tz[0:NW, :] = t
    tz[NW:, :] = t
    pl.semaphore_wait(barrier, n_peers + 1)

    def visit(v, carry):
        first = v == 0
        buf = field.at[v]
        paired = pair_copy(v)
        halo = halo_copies(v, buf, W, 1)
        near = z_copies(v, buf, own_box, 10)
        far = z_copies(v, buf, outer_boxes(W), 11)

        def q_halo():
            return halo_copies(v, qf, 1, 14)

        def q_near():
            return z_copies(v, qf, own_box, 23)

        def q_far():
            return z_copies(v, qf, outer_boxes(1), 24)

        start([paired] + halo[:2])

        @pl.when(first)
        def _():
            start(q_halo() + q_near())

        received([paired])
        gather(v)
        start(halo[2:] + near)
        received(halo)
        start(far)

        @pl.when(first)
        def _():
            received(q_halo())
            start(q_far())

        wait_rows(v, grecv)
        @pl.when(first)
        def _():
            lane = lax.broadcasted_iota(jnp.int32, (gxn * gyn, 128), 1)
            cond = pltpu.roll(coarse[v], 96, 1) * (1.0 / AGG**3)
            inv = one_f / jnp.where(lane < per * coln, cond, one_f)
            qcinv[...] = inv
            qcsel[...] = dot(dot(tab[16:32], inv), expand)
        t = dot(vyx[...], dot(coarse[v] * qcinv[...], vz[...])) * gain[...]
        expanded[...] = dot(dot(tab[0:16], t), vze[...]) * qcsel[...]
        e = expanded[...]
        for k in range(0, 9, 3):
            part[k // 3] = jnp.where(
                rows < NB, e[k + 1 : k + 2],
                jnp.where(rows < NB + 4, e[k + 2 : k + 3], e[k : k + 1]))

        received(near + far)

        def emit_one(s, b):
            one[s] = mask * slab_in(s) * (c1 * buf[s] + c2 * b)

        stencil(lambda s: mask * slab_in(s) * buf[s], emit_one, tz[...], 1, NS - 2, G1)

        def emit_two(s, b):
            k = jnp.where(s < W, 0, jnp.where(s >= W + NB, 2, 1))
            two[s] = mask * slab_in(s) * (c0 * buf[s] + b) + qf[s] * part[k]

        @pl.when(first)
        def _():
            received(q_near() + q_far())

        stencil(lambda s: one[s], emit_two, tz[...], W - 1, NB + 2, G2)

        sums[...] = jnp.zeros((NB, NL), jnp.float32)

        def emit_three(s, b):
            own = two[s, 0:NB, 0:NL]
            i = s - W
            rem = buf[s, 0:NB, 0:NL] - (8.0 + SHIFT) * own + 0.125 * b
            tot_ref[i] += own
            rem_ref[i] = rem
            field[v + 1, s, 0:NB, 0:NL] = rem
            sums[...] += rem * q[i]

        stencil(lambda s: two[s], emit_three, tz[:, 0:NL], W, NB, G3, NB)

        @pl.when(v < VISITS - 1)
        def _():
            pair[v + 1, 0:1, :] = block_row(sums[...])

        sent([paired] + halo + near + far)
        wait_rows(v, gsend)

        @pl.when(first)
        def _():
            sent(q_halo() + q_near() + q_far())

        return carry

    lax.fori_loop(0, VISITS, visit, 0)


def local(size, consts, source, conductance):
    gxn, gyn, coln = size
    n = gxn * gyn
    f32 = jnp.float32
    vmem = pltpu.VMEM
    dma = pltpu.SemaphoreType.DMA
    total, remainder = pl.pallas_call(
        functools.partial(kernel, size),
        out_shape=(vmem((NB, NB, NL), f32),) * 2,
        in_specs=[pl.BlockSpec(memory_space=pl.ANY)] * 6,
        out_specs=(pl.BlockSpec(memory_space=vmem),) * 2,
        scratch_shapes=[
            vmem((NB, NB, NL), f32),
            vmem((NB, NB, NL), f32),
            vmem((n, n), f32),
            vmem((128, 128), f32),
            vmem((n, 128), f32),
            vmem((32, n), f32),
            vmem((VISITS + 1, NS, NR, NW), f32),
            vmem((NS, NR, NW), f32),
            vmem((NS, NR, NW), f32),
            vmem((NS, NR, NW), f32),
            vmem((16, NW), f32),
            vmem((3, NR, NW), f32),
            vmem((NB, NL), f32),
            vmem((VISITS, 16, 128), f32),
            vmem((VISITS, n, 128), f32),
            vmem((n, 128), f32),
            vmem((16, NW), f32),
            vmem((128, NW), f32),
            vmem((2 * NW, NW), jnp.bfloat16),
            dma((6,)),
            dma((VISITS, 27)),
            dma((VISITS, 27)),
            dma((VISITS,)),
            dma((VISITS,)),
        ],
        compiler_params=pltpu.CompilerParams(
            collective_id=0, has_side_effects=True, vmem_limit_bytes=60 * 1024 * 1024
        ),
    )(source, conductance, *consts)
    return total / conductance, remainder * conductance


def solution(mesh):
    size = (mesh.shape["gx"], mesh.shape["gy"], mesh.shape["col"])
    consts = coarse_constants(size[0], size[1], NL // AGG * size[2])
    spec = P("gx", "gy", "col")
    return jax.shard_map(
        lambda a, b: local(size, [jnp.asarray(c) for c in consts], a, b),
        mesh=mesh,
        in_specs=(spec, spec),
        out_specs=(spec, spec),
        check_vma=False,
    )
```

```python
import functools
import math

import jax
import jax.numpy as jnp
import numpy as np
from jax import lax
from jax.experimental import pallas as pl
from jax.experimental.pallas import tpu as pltpu
from jax.sharding import PartitionSpec as P

AGG = 16
DEGREE = 3
VISITS = 3
CCYC = 4

SHIFT = 0.05
CENTER = 7.0 + SHIFT
UPPER = (8.0 + SHIFT) / CENTER
FINE_LOWER = UPPER / 4.0
COARSE_LOWER = SHIFT / CENTER
PROLONG = 0.5

NB = 16
NL = 256
W = 3
NS = NB + 2 * W
NR = 24
NW = 384
MESH = pl.DeviceIdType.MESH
G1, G2, G3 = 20, 18, 16
HALO_ORDER = ((None, 0), (None, 1), (0, 0), (0, 1), (1, 0), (1, 1), (0, None), (1, None))
HIGH = lax.Precision.HIGHEST


def cheb_poly(lower, upper):
    theta, delta = (upper + lower) / 2.0, (upper - lower) / 2.0
    sigma = theta / delta
    rho = 1.0 / sigma
    op = np.poly1d([-1.0, 8.0 + SHIFT])
    rem = np.poly1d([1.0])
    direction = rem * (1.0 / (CENTER * theta))
    total = direction
    for _ in range(DEGREE - 1):
        rem = rem - op * direction
        rho_new = 1.0 / (2.0 * sigma - rho)
        direction = (rho_new * rho) * direction + (2.0 * rho_new / delta / CENTER) * rem
        total = total + direction
        rho = rho_new
    return total


def coarse_gain(lam):
    c = cheb_poly(COARSE_LOWER, UPPER)(lam)
    err = np.zeros_like(lam)
    for _ in range(CCYC):
        err = err + c * (1.0 - (8.0 + SHIFT - lam) * err)
    return err


def sine(n):
    k = np.arange(1, n + 1)
    v = math.sqrt(2.0 / (n + 1)) * np.sin(np.pi * np.outer(k, k) / (n + 1))
    return v, 1.0 + np.cos(np.pi * k / (n + 1))


def coarse_constants(gx, gy, cz):
    vx, lx = sine(gx)
    vy, ly = sine(gy)
    vz, lz = sine(cz)
    order = [(x, y) for x in range(gx) for y in range(gy)]
    xs = np.array([o[0] for o in order])
    ys = np.array([o[1] for o in order])
    n = len(order)
    vyx = vx[np.ix_(xs, xs)] * vy[np.ix_(ys, ys)]
    lam = (lx[xs] * ly[ys])[:, None] * lz[None, :]
    gain = np.zeros((n, 128))
    gain[:, :cz] = PROLONG * AGG ** (-1.5) * coarse_gain(lam)
    vzp = np.zeros((128, 128))
    vzp[:cz, :cz] = vz
    where = {o: i for i, o in enumerate(order)}
    table = np.zeros((gx, gy, 32, n))
    for x in range(gx):
        for y in range(gy):
            for dx in range(3):
                for dy in range(3):
                    at = where.get((x + dx - 1, y + dy - 1))
                    if at is not None:
                        table[x, y, dx * 3 + dy] = vyx[at]
                        table[x, y, 16 + dx * 3 + dy, at] = 1.0
    f32 = np.float32
    return vyx.astype(f32), vzp.astype(f32), gain.astype(f32), table.reshape(gx * gy, 32, n).astype(f32)


def dot(a, b):
    return jnp.dot(a, b, precision=HIGH, preferred_element_type=jnp.float32)


def halves(v):
    high = v.astype(jnp.bfloat16)
    return high, (v - high.astype(jnp.float32)).astype(jnp.bfloat16)


def right(v):
    high, low = halves(v)
    return jnp.concatenate([high, high, low], axis=0)


def left(v):
    high, low = halves(v)
    return jnp.concatenate([high, high, low], axis=1)


def data_left(v):
    high, low = halves(v)
    return jnp.concatenate([high, low, high], axis=1)


def data_right(v):
    high, low = halves(v)
    return jnp.concatenate([high, low, high], axis=0)


def dot3(a, b):
    return jnp.dot(a, b, preferred_element_type=jnp.float32)


def y_sum(v):
    v = v + pltpu.roll(v, v.shape[0] - 1, 0)
    return v + pltpu.roll(v, 1, 0)


def z_matrix():
    i = lax.broadcasted_iota(jnp.int32, (NW, NW), 0)
    j = lax.broadcasted_iota(jnp.int32, (NW, NW), 1)
    d = jnp.abs(i - j)
    return jnp.where(d == 0, 2.0, jnp.where((d == 1) | (d == NW - 1), 1.0, 0.0)).astype(jnp.bfloat16)


def z_sum(v, tz):
    high = v.astype(jnp.bfloat16)
    low = (v - high.astype(jnp.float32)).astype(jnp.bfloat16)
    return jnp.dot(jnp.concatenate([high, low], axis=1), tz, preferred_element_type=jnp.float32)


def stencil(load, emit, tz, first, count, group, rows=NR):
    here = load(first)

    def body(i, carry):
        pair, here = carry
        out = []
        for k in range(group):
            after = load(first + i * group + k + 1)
            pair_after = here + after
            out.append(y_sum(pair + pair_after)[:rows])
            pair, here = pair_after, after
        out = z_sum(jnp.concatenate(out, axis=0), tz)
        for k in range(group):
            emit(first + i * group + k, out[k * rows : (k + 1) * rows])
        return pair, here

    carry = (load(first - 1) + here, here)
    if group == count:
        body(0, carry)
    else:
        lax.fori_loop(0, count // group, body, carry)


def far_first(ny):
    def ring(d, n):
        return min(d, n - d)

    every = [(dy, dx) for dy in range(ny) for dx in range(4)]
    return sorted(every, key=lambda d: (-ring(d[0], ny) - ring(d[1], 4), d))


def kernel(
    size,
    src_hbm, q_hbm, vyx_hbm, vz_hbm, gain_hbm, tab_hbm,
    tot_ref, rem_ref,
    src, q, vyx, vz, gain, tab,
    field, qf, one, two, expanded, part, sums,
    pair, coarse, qcinv, qcsel, vze3, vz3, vyx3, tab3, place2, tz,
    lsem, hsend, hrecv, gsend, grecv,
):
    gxn, gyn, coln = size
    gx, gy, col = lax.axis_index("gx"), lax.axis_index("gy"), lax.axis_index("col")
    other = 1 - col
    me = gx * gyn + gy
    poly = cheb_poly(FINE_LOWER, UPPER).coeffs
    c2, c1, c0 = (float(c) * 8.0**-k for c, k in zip(poly, (2, 1, 0)))

    local_copies = [
        pltpu.make_async_copy(a, b, lsem.at[k])
        for k, (a, b) in enumerate((
            (src_hbm, src), (q_hbm, q), (tab_hbm.at[me], tab),
            (vyx_hbm, vyx), (vz_hbm, vz), (gain_hbm, gain)))
    ]
    for c in local_copies:
        c.start()

    nz, ny = gxn // 2, gyn // 2
    z, y, x = gx // 2, gy // 2, lax.rem(gy, 2) * 2 + lax.rem(gx, 2)
    y_of = [lax.rem(y + d, ny) * 2 for d in range(ny)]
    x_of = [lax.rem(x + d, 4) for d in range(4)]
    lo_of, hi_of = [lax.rem(a, 2) for a in x_of], [a // 2 for a in x_of]
    plane = far_first(ny)
    n_peers = nz * ny * 4 - 1

    def each_peer(act):
        def planes(k, carry):
            dz = nz // 2 + jnp.where(lax.rem(k, 2) == 0, k // 2, -((k + 1) // 2))
            z_of = lax.rem(z + dz, nz) * 2
            for dy, dx in plane:
                act((z_of + lo_of[dx], y_of[dy] + hi_of[dx], col))
            return carry

        lax.fori_loop(0, nz - 1, planes, 0)
        for dy, dx in plane:
            if dy or dx:
                act((z * 2 + lo_of[dx], y_of[dy] + hi_of[dx], col))

    sibling = (gx, gy, other)

    barrier = pltpu.get_barrier_semaphore()

    def greet(p):
        pl.semaphore_signal(barrier, inc=1, device_id=p, device_id_type=MESH)

    each_peer(greet)
    greet(sibling)

    xs = (lax.rem(gx + gxn - 1, gxn), lax.rem(gx + 1, gxn))
    ys = (lax.rem(gy + gyn - 1, gyn), lax.rem(gy + 1, gyn))

    one_f = jnp.float32(1.0)
    zero_f = jnp.float32(0.0)
    x_in = (jnp.where(gx > 0, one_f, zero_f), jnp.where(gx < gxn - 1, one_f, zero_f))
    y_in = (jnp.where(gy > 0, one_f, zero_f), jnp.where(gy < gyn - 1, one_f, zero_f))
    rows = lax.broadcasted_iota(jnp.int32, (NR, NW), 0)
    lanes = lax.broadcasted_iota(jnp.int32, (NR, NW), 1)
    first_z = jnp.where(col == 0, NL, NW - 4)
    row_mask = jnp.where(rows < NB, one_f, jnp.where(rows < NB + 4, y_in[1], y_in[0]))
    lane_mask = jnp.where((lanes < NL) | ((lanes >= first_z) & (lanes < first_z + 4)), one_f, zero_f)
    mask = row_mask * lane_mask

    def slab_in(s):
        return jnp.where(s < W, x_in[0], jnp.where(s >= W + NB, x_in[1], one_f))

    per = NL // AGG
    zi = lax.broadcasted_iota(jnp.int32, (NL, 128), 0) // AGG + col * per
    li = lax.broadcasted_iota(jnp.int32, (NL, 128), 1)
    place = jnp.where(li == zi, one_f, zero_f)
    ki = lax.broadcasted_iota(jnp.int32, (128, NW), 0)
    ci = lax.broadcasted_iota(jnp.int32, (128, NW), 1)
    coarse_of = jnp.where(
        ci < NL, col * per + ci // AGG, jnp.where(col == 0, per, per - 1)
    )
    valid = (ci < NL) | ((ci >= first_z) & (ci < first_z + 4))
    expand = jnp.where((ki == coarse_of) & valid, one_f, zero_f)

    def block_row(acc):
        parts = jnp.concatenate(halves(acc[:8] + acc[8:]), axis=1)
        return jnp.sum(dot3(parts, place2[...]), axis=0, keepdims=True)

    def remote(src_ref, dst_ref, send, recv, to):
        return pltpu.make_async_remote_copy(
            src_ref=src_ref, dst_ref=dst_ref, send_sem=send, recv_sem=recv,
            device_id=to, device_id_type=MESH,
        )

    def start(copies):
        for c in copies:
            c.start()

    def received(copies):
        for c in copies:
            c.wait_recv()

    def sent(copies):
        for c in copies:
            c.wait_send()

    def pair_copy(v):
        return remote(pair.at[v, pl.ds(0, 1)], pair.at[v, pl.ds(8, 1)], hsend.at[v, 0], hrecv.at[v, 0], sibling)

    def gather(v):
        mine = coarse.at[v, pl.ds(me, 1)]
        mine[...] = pair[v, 0:1, :] + pair[v, 8:9, :]
        each_peer(lambda p: remote(mine, mine, gsend.at[v], grecv.at[v], p).start())

    def wait_rows(v, sem):
        ref = coarse.at[v, pl.ds(0, n_peers)]
        pltpu.make_async_copy(ref, ref, sem.at[v]).wait()

    def halo_copies(v, buf, width, base):
        copies = []
        slabs = ((W, W + NB), (W + NB - width, W - width))
        lines = ((0, NB), (NB - width, NR - width))
        for a, b in HALO_ORDER:
            s0, s1, sn = (W, W, NB) if a is None else slabs[a] + (width,)
            r0, r1, rn = (0, 0, NB) if b is None else lines[b] + (width,)
            to = (gx if a is None else xs[a], gy if b is None else ys[b], col)
            code = lambda a, b: base + (2 if a is None else a) * 3 + (2 if b is None else b)
            there = code(None if a is None else 1 - a, None if b is None else 1 - b)
            copies.append(remote(
                buf.at[pl.ds(s0, sn), pl.ds(r0, rn), pl.ds(0, NL)],
                buf.at[pl.ds(s1, sn), pl.ds(r1, rn), pl.ds(0, NL)],
                hsend.at[v, code(a, b)], hrecv.at[v, there], to))
        return copies

    inner = pl.multiple_of(other * 128, 128)

    def z_copies(v, buf, boxes, base):
        copies = []
        for k, (s, sn, r, rn) in enumerate(boxes):
            copies.append(remote(
                buf.at[pl.ds(s, sn), pl.ds(r, rn), pl.ds(inner, 128)],
                buf.at[pl.ds(s, sn), pl.ds(r, rn), pl.ds(NL, 128)],
                hsend.at[v, base + k], hrecv.at[v, base + k], sibling))
        return copies

    own_box = [(W, NB, 0, NB)]

    def outer_boxes(width):
        return [(W, NB, NB, NR - NB), (W - width, width, 0, NR), (W + NB, width, 0, NR)]

    half = place.astype(jnp.bfloat16)
    place2[0:NL, :] = half
    place2[NL:, :] = half
    local_copies[0].wait()
    local_copies[1].wait()
    rhs_acc = jnp.zeros((NB, NL), jnp.float32)
    cond_acc = jnp.zeros((NB, NL), jnp.float32)
    for s in range(NB):
        rhs_acc = rhs_acc + src[s]
        cond_acc = cond_acc + q[s]
    pair[0, 0:1, :] = block_row(rhs_acc) + pltpu.roll(block_row(cond_acc), 32, 1)
    for s in range(NB):
        field[0, W + s, 0:NB, 0:NL] = src[s] / q[s]
        qf[W + s, 0:NB, 0:NL] = q[s]
        tot_ref[s] = jnp.zeros((NB, NL), jnp.float32)
    for c in local_copies[2:]:
        c.wait()
    vze3[...] = right(dot(vz[...], expand))
    vz3[...] = right(vz[...])
    vyx3[...] = left(vyx[...])
    tab3[...] = left(tab[0:16])
    t = z_matrix()
    tz[0:NW, :] = t
    tz[NW:, :] = t
    pl.semaphore_wait(barrier, n_peers + 1)

    def visit(v, carry):
        first = v == 0
        buf = field.at[v]
        paired = pair_copy(v)
        halo = halo_copies(v, buf, W, 1)
        near = z_copies(v, buf, own_box, 10)
        far = z_copies(v, buf, outer_boxes(W), 11)

        def q_halo():
            return halo_copies(v, qf, 1, 14)

        def q_near():
            return z_copies(v, qf, own_box, 23)

        def q_far():
            return z_copies(v, qf, outer_boxes(1), 24)

        start([paired] + halo[:2])

        @pl.when(first)
        def _():
            start(q_halo() + q_near())

        received([paired])
        gather(v)
        start(halo[2:] + near)
        received(halo)
        start(far)

        @pl.when(first)
        def _():
            received(q_halo())
            start(q_far())

        wait_rows(v, grecv)
        @pl.when(first)
        def _():
            lane = lax.broadcasted_iota(jnp.int32, (gxn * gyn, 128), 1)
            cond = pltpu.roll(coarse[v], 96, 1) * (1.0 / AGG**3)
            inv = one_f / jnp.where(lane < per * coln, cond, one_f)
            qcinv[...] = inv
            qcsel[...] = dot(dot(tab[16:32], inv), expand)
        t = dot3(data_left(coarse[v] * qcinv[...]), vz3[...])
        t = dot3(vyx3[...], data_right(t)) * gain[...]
        t = dot3(tab3[...], data_right(t))
        expanded[...] = dot3(data_left(t), vze3[...]) * qcsel[...]
        e = expanded[...]
        for k in range(0, 9, 3):
            part[k // 3] = jnp.where(
                rows < NB, e[k + 1 : k + 2],
                jnp.where(rows < NB + 4, e[k + 2 : k + 3], e[k : k + 1]))

        received(near + far)

        def emit_one(s, b):
            one[s] = mask * slab_in(s) * (c1 * buf[s] + c2 * b)

        stencil(lambda s: mask * slab_in(s) * buf[s], emit_one, tz[...], 1, NS - 2, G1)

        def emit_two(s, b):
            k = jnp.where(s < W, 0, jnp.where(s >= W + NB, 2, 1))
            two[s] = mask * slab_in(s) * (c0 * buf[s] + b) + qf[s] * part[k]

        @pl.when(first)
        def _():
            received(q_near() + q_far())

        stencil(lambda s: one[s], emit_two, tz[...], W - 1, NB + 2, G2)

        sums[...] = jnp.zeros((NB, NL), jnp.float32)

        def emit_three(s, b):
            own = two[s, 0:NB, 0:NL]
            i = s - W
            rem = buf[s, 0:NB, 0:NL] - (8.0 + SHIFT) * own + 0.125 * b
            tot_ref[i] += own
            rem_ref[i] = rem
            field[v + 1, s, 0:NB, 0:NL] = rem
            sums[...] += rem * q[i]

        stencil(lambda s: two[s], emit_three, tz[:, 0:NL], W, NB, G3, NB)

        @pl.when(v < VISITS - 1)
        def _():
            pair[v + 1, 0:1, :] = block_row(sums[...])

        sent([paired] + halo + near + far)
        wait_rows(v, gsend)

        @pl.when(first)
        def _():
            sent(q_halo() + q_near() + q_far())

        return carry

    lax.fori_loop(0, VISITS, visit, 0)


def local(size, consts, source, conductance):
    gxn, gyn, coln = size
    n = gxn * gyn
    f32 = jnp.float32
    vmem = pltpu.VMEM
    dma = pltpu.SemaphoreType.DMA
    total, remainder = pl.pallas_call(
        functools.partial(kernel, size),
        out_shape=(vmem((NB, NB, NL), f32),) * 2,
        in_specs=[pl.BlockSpec(memory_space=pl.ANY)] * 6,
        out_specs=(pl.BlockSpec(memory_space=vmem),) * 2,
        scratch_shapes=[
            vmem((NB, NB, NL), f32),
            vmem((NB, NB, NL), f32),
            vmem((n, n), f32),
            vmem((128, 128), f32),
            vmem((n, 128), f32),
            vmem((32, n), f32),
            vmem((VISITS + 1, NS, NR, NW), f32),
            vmem((NS, NR, NW), f32),
            vmem((NS, NR, NW), f32),
            vmem((NS, NR, NW), f32),
            vmem((16, NW), f32),
            vmem((3, NR, NW), f32),
            vmem((NB, NL), f32),
            vmem((VISITS, 16, 128), f32),
            vmem((VISITS, n, 128), f32),
            vmem((n, 128), f32),
            vmem((16, NW), f32),
            vmem((384, NW), jnp.bfloat16),
            vmem((384, 128), jnp.bfloat16),
            vmem((n, 3 * n), jnp.bfloat16),
            vmem((16, 3 * n), jnp.bfloat16),
            vmem((2 * NL, 128), jnp.bfloat16),
            vmem((2 * NW, NW), jnp.bfloat16),
            dma((6,)),
            dma((VISITS, 27)),
            dma((VISITS, 27)),
            dma((VISITS,)),
            dma((VISITS,)),
        ],
        compiler_params=pltpu.CompilerParams(
            collective_id=0, has_side_effects=True, vmem_limit_bytes=60 * 1024 * 1024
        ),
    )(source, conductance, *consts)
    return total / conductance, remainder * conductance


def solution(mesh):
    size = (mesh.shape["gx"], mesh.shape["gy"], mesh.shape["col"])
    consts = coarse_constants(size[0], size[1], NL // AGG * size[2])
    spec = P("gx", "gy", "col")
    return jax.shard_map(
        lambda a, b: local(size, [jnp.asarray(c) for c in consts], a, b),
        mesh=mesh,
        in_specs=(spec, spec),
        out_specs=(spec, spec),
        check_vma=False,
    )
```

```python
import functools
import math

import jax
import jax.numpy as jnp
import numpy as np
from jax import lax
from jax.experimental import pallas as pl
from jax.experimental.pallas import tpu as pltpu
from jax.sharding import PartitionSpec as P

AGG = 16
DEGREE = 3
VISITS = 3
CCYC = 4

SHIFT = 0.05
CENTER = 7.0 + SHIFT
UPPER = (8.0 + SHIFT) / CENTER
FINE_LOWER = UPPER / 4.0
COARSE_LOWER = SHIFT / CENTER
PROLONG = 0.5

NB = 16
NL = 256
W = 3
NS = NB + 2 * W
NR = 24
NW = 384
MESH = pl.DeviceIdType.MESH
G1, G2, G3 = 20, 18, 16
HALO_ORDER = ((None, 0), (None, 1), (0, 0), (0, 1), (1, 0), (1, 1), (0, None), (1, None))
HIGH = lax.Precision.HIGHEST


def cheb_poly(lower, upper):
    theta, delta = (upper + lower) / 2.0, (upper - lower) / 2.0
    sigma = theta / delta
    rho = 1.0 / sigma
    op = np.poly1d([-1.0, 8.0 + SHIFT])
    rem = np.poly1d([1.0])
    direction = rem * (1.0 / (CENTER * theta))
    total = direction
    for _ in range(DEGREE - 1):
        rem = rem - op * direction
        rho_new = 1.0 / (2.0 * sigma - rho)
        direction = (rho_new * rho) * direction + (2.0 * rho_new / delta / CENTER) * rem
        total = total + direction
        rho = rho_new
    return total


def coarse_gain(lam):
    c = cheb_poly(COARSE_LOWER, UPPER)(lam)
    err = np.zeros_like(lam)
    for _ in range(CCYC):
        err = err + c * (1.0 - (8.0 + SHIFT - lam) * err)
    return err


def sine(n):
    k = np.arange(1, n + 1)
    v = math.sqrt(2.0 / (n + 1)) * np.sin(np.pi * np.outer(k, k) / (n + 1))
    return v, 1.0 + np.cos(np.pi * k / (n + 1))


def coarse_constants(gx, gy, cz):
    vx, lx = sine(gx)
    vy, ly = sine(gy)
    vz, lz = sine(cz)
    order = [(x, y) for x in range(gx) for y in range(gy)]
    xs = np.array([o[0] for o in order])
    ys = np.array([o[1] for o in order])
    n = len(order)
    vyx = vx[np.ix_(xs, xs)] * vy[np.ix_(ys, ys)]
    lam = (lx[xs] * ly[ys])[:, None] * lz[None, :]
    gain = np.zeros((n, 128))
    gain[:, :cz] = PROLONG * AGG ** (-1.5) * coarse_gain(lam)
    vzp = np.zeros((128, 128))
    vzp[:cz, :cz] = vz
    where = {o: i for i, o in enumerate(order)}
    table = np.zeros((gx, gy, 32, n))
    for x in range(gx):
        for y in range(gy):
            for dx in range(3):
                for dy in range(3):
                    at = where.get((x + dx - 1, y + dy - 1))
                    if at is not None:
                        table[x, y, dx * 3 + dy] = vyx[at]
                        table[x, y, 16 + dx * 3 + dy, at] = 1.0
    f32 = np.float32
    return vyx.astype(f32), vzp.astype(f32), gain.astype(f32), table.reshape(gx * gy, 32, n).astype(f32)


def dot(a, b):
    return jnp.dot(a, b, precision=HIGH, preferred_element_type=jnp.float32)


def halves(v):
    high = v.astype(jnp.bfloat16)
    return high, (v - high.astype(jnp.float32)).astype(jnp.bfloat16)


def right(v):
    high, low = halves(v)
    return jnp.concatenate([high, high, low], axis=0)


def left(v):
    high, low = halves(v)
    return jnp.concatenate([high, high, low], axis=1)


def data_left(v):
    high, low = halves(v)
    return jnp.concatenate([high, low, high], axis=1)


def data_right(v):
    high, low = halves(v)
    return jnp.concatenate([high, low, high], axis=0)


def dot3(a, b):
    return jnp.dot(a, b, preferred_element_type=jnp.float32)


def y_sum(v):
    v = v + pltpu.roll(v, v.shape[0] - 1, 0)
    return v + pltpu.roll(v, 1, 0)


def z_matrix():
    i = lax.broadcasted_iota(jnp.int32, (NW, NW), 0)
    j = lax.broadcasted_iota(jnp.int32, (NW, NW), 1)
    d = jnp.abs(i - j)
    return jnp.where(d == 0, 2.0, jnp.where((d == 1) | (d == NW - 1), 1.0, 0.0)).astype(jnp.bfloat16)


def z_sum(v, tz):
    high = v.astype(jnp.bfloat16)
    low = (v - high.astype(jnp.float32)).astype(jnp.bfloat16)
    return jnp.dot(jnp.concatenate([high, low], axis=1), tz, preferred_element_type=jnp.float32)


def stencil(load, emit, tz, first, count, group, rows=NR):
    here = load(first)

    def body(i, carry):
        pair, here = carry
        out = []
        for k in range(group):
            after = load(first + i * group + k + 1)
            pair_after = here + after
            out.append(y_sum(pair + pair_after)[:rows])
            pair, here = pair_after, after
        out = z_sum(jnp.concatenate(out, axis=0), tz)
        for k in range(group):
            emit(first + i * group + k, out[k * rows : (k + 1) * rows])
        return pair, here

    carry = (load(first - 1) + here, here)
    if group == count:
        body(0, carry)
    else:
        lax.fori_loop(0, count // group, body, carry)


def far_first(ny):
    def ring(d, n):
        return min(d, n - d)

    every = [(dy, dx) for dy in range(ny) for dx in range(4)]
    return sorted(every, key=lambda d: (-ring(d[0], ny) - ring(d[1], 4), d))


def kernel(
    size,
    src_hbm, q_hbm, vyx_hbm, vz_hbm, gain_hbm, tab_hbm,
    tot_ref, rem_ref,
    src, q, vyx, vz, gain, tab,
    field, qf, one, two, expanded, part, sums,
    pair, coarse, qcinv, qcsel, vze3, vz3, vyx3, tab3, place2, tz,
    lsem, hsend, hrecv, gsend, grecv,
):
    gxn, gyn, coln = size
    gx, gy, col = lax.axis_index("gx"), lax.axis_index("gy"), lax.axis_index("col")
    other = 1 - col
    me = gx * gyn + gy
    poly = cheb_poly(FINE_LOWER, UPPER).coeffs
    c2, c1, c0 = (float(c) * 8.0**-k for c, k in zip(poly, (2, 1, 0)))

    local_copies = [
        pltpu.make_async_copy(a, b, lsem.at[k])
        for k, (a, b) in enumerate((
            (src_hbm, src), (q_hbm, q), (tab_hbm.at[me], tab),
            (vyx_hbm, vyx), (vz_hbm, vz), (gain_hbm, gain)))
    ]
    for c in local_copies:
        c.start()

    nz, ny = gxn // 2, gyn // 2
    z, y, x = gx // 2, gy // 2, lax.rem(gy, 2) * 2 + lax.rem(gx, 2)
    y_of = [lax.rem(y + d, ny) * 2 for d in range(ny)]
    x_of = [lax.rem(x + d, 4) for d in range(4)]
    lo_of, hi_of = [lax.rem(a, 2) for a in x_of], [a // 2 for a in x_of]
    plane = far_first(ny)
    n_peers = nz * ny * 4 - 1

    def each_peer(act):
        def planes(k, carry):
            dz = nz // 2 + jnp.where(lax.rem(k, 2) == 0, k // 2, -((k + 1) // 2))
            z_of = lax.rem(z + dz, nz) * 2
            for dy, dx in plane:
                act((z_of + lo_of[dx], y_of[dy] + hi_of[dx], col))
            return carry

        lax.fori_loop(0, nz - 1, planes, 0)
        for dy, dx in plane:
            if dy or dx:
                act((z * 2 + lo_of[dx], y_of[dy] + hi_of[dx], col))

    sibling = (gx, gy, other)

    barrier = pltpu.get_barrier_semaphore()

    def greet(p):
        pl.semaphore_signal(barrier, inc=1, device_id=p, device_id_type=MESH)

    each_peer(greet)
    greet(sibling)

    xs = (lax.rem(gx + gxn - 1, gxn), lax.rem(gx + 1, gxn))
    ys = (lax.rem(gy + gyn - 1, gyn), lax.rem(gy + 1, gyn))

    one_f = jnp.float32(1.0)
    zero_f = jnp.float32(0.0)
    x_in = (jnp.where(gx > 0, one_f, zero_f), jnp.where(gx < gxn - 1, one_f, zero_f))
    y_in = (jnp.where(gy > 0, one_f, zero_f), jnp.where(gy < gyn - 1, one_f, zero_f))
    rows = lax.broadcasted_iota(jnp.int32, (NR, NW), 0)
    lanes = lax.broadcasted_iota(jnp.int32, (NR, NW), 1)
    first_z = jnp.where(col == 0, NL, NW - 4)
    row_mask = jnp.where(rows < NB, one_f, jnp.where(rows < NB + 4, y_in[1], y_in[0]))
    lane_mask = jnp.where((lanes < NL) | ((lanes >= first_z) & (lanes < first_z + 4)), one_f, zero_f)
    mask = row_mask * lane_mask

    def slab_in(s):
        return jnp.where(s < W, x_in[0], jnp.where(s >= W + NB, x_in[1], one_f))

    per = NL // AGG
    zi = lax.broadcasted_iota(jnp.int32, (NL, 128), 0) // AGG + col * per
    li = lax.broadcasted_iota(jnp.int32, (NL, 128), 1)
    place = jnp.where(li == zi, one_f, zero_f)
    ki = lax.broadcasted_iota(jnp.int32, (128, NW), 0)
    ci = lax.broadcasted_iota(jnp.int32, (128, NW), 1)
    coarse_of = jnp.where(
        ci < NL, col * per + ci // AGG, jnp.where(col == 0, per, per - 1)
    )
    valid = (ci < NL) | ((ci >= first_z) & (ci < first_z + 4))
    expand = jnp.where((ki == coarse_of) & valid, one_f, zero_f)

    def block_row(acc):
        parts = jnp.concatenate(halves(acc[:8] + acc[8:]), axis=1)
        return jnp.sum(dot3(parts, place2[...]), axis=0, keepdims=True)

    def remote(src_ref, dst_ref, send, recv, to):
        return pltpu.make_async_remote_copy(
            src_ref=src_ref, dst_ref=dst_ref, send_sem=send, recv_sem=recv,
            device_id=to, device_id_type=MESH,
        )

    def start(copies):
        for c in copies:
            c.start()

    def received(copies):
        for c in copies:
            c.wait_recv()

    def sent(copies):
        for c in copies:
            c.wait_send()

    def pair_copy(v):
        return remote(pair.at[v, pl.ds(0, 1)], pair.at[v, pl.ds(8, 1)], hsend.at[v, 0], hrecv.at[v, 0], sibling)

    def gather(v):
        mine = coarse.at[v, pl.ds(me, 1)]
        mine[...] = pair[v, 0:1, :] + pair[v, 8:9, :]
        each_peer(lambda p: remote(mine, mine, gsend.at[v], grecv.at[v], p).start())

    def wait_rows(v, sem):
        ref = coarse.at[v, pl.ds(0, n_peers)]
        pltpu.make_async_copy(ref, ref, sem.at[v]).wait()

    def halo_copies(v, buf, width, base):
        copies = []
        slabs = ((W, W + NB), (W + NB - width, W - width))
        lines = ((0, NB), (NB - width, NR - width))
        for a, b in HALO_ORDER:
            s0, s1, sn = (W, W, NB) if a is None else slabs[a] + (width,)
            r0, r1, rn = (0, 0, NB) if b is None else lines[b] + (width,)
            to = (gx if a is None else xs[a], gy if b is None else ys[b], col)
            code = lambda a, b: base + (2 if a is None else a) * 3 + (2 if b is None else b)
            there = code(None if a is None else 1 - a, None if b is None else 1 - b)
            copies.append(remote(
                buf.at[pl.ds(s0, sn), pl.ds(r0, rn), pl.ds(0, NL)],
                buf.at[pl.ds(s1, sn), pl.ds(r1, rn), pl.ds(0, NL)],
                hsend.at[v, code(a, b)], hrecv.at[v, there], to))
        return copies

    inner = pl.multiple_of(other * 128, 128)

    def z_copies(v, buf, boxes, base):
        copies = []
        for k, (s, sn, r, rn) in enumerate(boxes):
            copies.append(remote(
                buf.at[pl.ds(s, sn), pl.ds(r, rn), pl.ds(inner, 128)],
                buf.at[pl.ds(s, sn), pl.ds(r, rn), pl.ds(NL, 128)],
                hsend.at[v, base + k], hrecv.at[v, base + k], sibling))
        return copies

    own_box = [(W, NB, 0, NB)]

    def outer_boxes(width):
        return [(W, NB, NB, NR - NB), (W - width, width, 0, NR), (W + NB, width, 0, NR)]

    half = place.astype(jnp.bfloat16)
    place2[0:NL, :] = half
    place2[NL:, :] = half
    local_copies[0].wait()
    local_copies[1].wait()
    rhs_acc = jnp.zeros((NB, NL), jnp.float32)
    cond_acc = jnp.zeros((NB, NL), jnp.float32)
    for s in range(NB):
        rhs_acc = rhs_acc + src[s]
        cond_acc = cond_acc + q[s]
    pair[0, 0:1, :] = block_row(rhs_acc) + pltpu.roll(block_row(cond_acc), 32, 1)
    for s in range(NB):
        field[0, W + s, 0:NB, 0:NL] = src[s] / q[s]
        qf[W + s, 0:NB, 0:NL] = q[s]
        tot_ref[s] = jnp.zeros((NB, NL), jnp.float32)
    for c in local_copies[2:]:
        c.wait()
    vze3[...] = right(dot(vz[...], expand))
    vz3[...] = right(vz[...])
    vyx3[...] = left(vyx[...])
    tab3[...] = left(tab[0:16])
    t = z_matrix()
    tz[0:NW, :] = t
    tz[NW:, :] = t
    pl.semaphore_wait(barrier, n_peers + 1)

    def visit(v, carry):
        first = v == 0
        buf = field.at[v]
        paired = pair_copy(v)
        halo = halo_copies(v, buf, W, 1)
        near = z_copies(v, buf, own_box, 10)
        far = z_copies(v, buf, outer_boxes(W), 11)

        def q_halo():
            return halo_copies(v, qf, 1, 14)

        def q_near():
            return z_copies(v, qf, own_box, 23)

        def q_far():
            return z_copies(v, qf, outer_boxes(1), 24)

        start([paired] + halo[:2])

        @pl.when(first)
        def _():
            start(q_halo() + q_near())

        received([paired])
        gather(v)
        start(halo[2:] + near)
        received(halo)
        start(far)

        @pl.when(first)
        def _():
            received(q_halo())
            start(q_far())

        wait_rows(v, grecv)
        @pl.when(first)
        def _():
            lane = lax.broadcasted_iota(jnp.int32, (gxn * gyn, 128), 1)
            cond = pltpu.roll(coarse[v], 96, 1) * (1.0 / AGG**3)
            inv = one_f / jnp.where(lane < per * coln, cond, one_f)
            qcinv[...] = inv
            pick = tab[16:32].astype(jnp.bfloat16)
            near_inv = dot3(jnp.concatenate([pick, pick], axis=1), jnp.concatenate(halves(inv), axis=0))
            spread = expand.astype(jnp.bfloat16)
            qcsel[...] = dot3(
                jnp.concatenate(halves(near_inv), axis=1), jnp.concatenate([spread, spread], axis=0))
        t = dot3(data_left(coarse[v] * qcinv[...]), vz3[...])
        t = dot3(vyx3[...], data_right(t)) * gain[...]
        t = dot3(tab3[...], data_right(t))
        expanded[...] = dot3(data_left(t), vze3[...]) * qcsel[...]
        e = expanded[...]
        for k in range(0, 9, 3):
            part[k // 3] = jnp.where(
                rows < NB, e[k + 1 : k + 2],
                jnp.where(rows < NB + 4, e[k + 2 : k + 3], e[k : k + 1]))

        received(near + far)

        def emit_one(s, b):
            one[s] = mask * slab_in(s) * (c1 * buf[s] + c2 * b)

        stencil(lambda s: mask * slab_in(s) * buf[s], emit_one, tz[...], 1, NS - 2, G1)

        def emit_two(s, b):
            k = jnp.where(s < W, 0, jnp.where(s >= W + NB, 2, 1))
            two[s] = mask * slab_in(s) * (c0 * buf[s] + b) + qf[s] * part[k]

        @pl.when(first)
        def _():
            received(q_near() + q_far())

        stencil(lambda s: one[s], emit_two, tz[...], W - 1, NB + 2, G2)

        sums[...] = jnp.zeros((NB, NL), jnp.float32)

        def emit_three(s, b):
            own = two[s, 0:NB, 0:NL]
            i = s - W
            rem = buf[s, 0:NB, 0:NL] - (8.0 + SHIFT) * own + 0.125 * b
            tot_ref[i] += own
            rem_ref[i] = rem
            field[v + 1, s, 0:NB, 0:NL] = rem
            sums[...] += rem * q[i]

        stencil(lambda s: two[s], emit_three, tz[:, 0:NL], W, NB, G3, NB)

        @pl.when(v < VISITS - 1)
        def _():
            pair[v + 1, 0:1, :] = block_row(sums[...])

        sent([paired] + halo + near + far)
        wait_rows(v, gsend)

        @pl.when(first)
        def _():
            sent(q_halo() + q_near() + q_far())

        return carry

    lax.fori_loop(0, VISITS, visit, 0)


def local(size, consts, source, conductance):
    gxn, gyn, coln = size
    n = gxn * gyn
    f32 = jnp.float32
    vmem = pltpu.VMEM
    dma = pltpu.SemaphoreType.DMA
    total, remainder = pl.pallas_call(
        functools.partial(kernel, size),
        out_shape=(vmem((NB, NB, NL), f32),) * 2,
        in_specs=[pl.BlockSpec(memory_space=pl.ANY)] * 6,
        out_specs=(pl.BlockSpec(memory_space=vmem),) * 2,
        scratch_shapes=[
            vmem((NB, NB, NL), f32),
            vmem((NB, NB, NL), f32),
            vmem((n, n), f32),
            vmem((128, 128), f32),
            vmem((n, 128), f32),
            vmem((32, n), f32),
            vmem((VISITS + 1, NS, NR, NW), f32),
            vmem((NS, NR, NW), f32),
            vmem((NS, NR, NW), f32),
            vmem((NS, NR, NW), f32),
            vmem((16, NW), f32),
            vmem((3, NR, NW), f32),
            vmem((NB, NL), f32),
            vmem((VISITS, 16, 128), f32),
            vmem((VISITS, n, 128), f32),
            vmem((n, 128), f32),
            vmem((16, NW), f32),
            vmem((384, NW), jnp.bfloat16),
            vmem((384, 128), jnp.bfloat16),
            vmem((n, 3 * n), jnp.bfloat16),
            vmem((16, 3 * n), jnp.bfloat16),
            vmem((2 * NL, 128), jnp.bfloat16),
            vmem((2 * NW, NW), jnp.bfloat16),
            dma((6,)),
            dma((VISITS, 27)),
            dma((VISITS, 27)),
            dma((VISITS,)),
            dma((VISITS,)),
        ],
        compiler_params=pltpu.CompilerParams(
            collective_id=0, has_side_effects=True, vmem_limit_bytes=60 * 1024 * 1024
        ),
    )(source, conductance, *consts)
    return total / conductance, remainder * conductance


def solution(mesh):
    size = (mesh.shape["gx"], mesh.shape["gy"], mesh.shape["col"])
    consts = coarse_constants(size[0], size[1], NL // AGG * size[2])
    spec = P("gx", "gy", "col")
    return jax.shard_map(
        lambda a, b: local(size, [jnp.asarray(c) for c in consts], a, b),
        mesh=mesh,
        in_specs=(spec, spec),
        out_specs=(spec, spec),
        check_vma=False,
    )
```
